128 devices in a mesh: struct: 32 (over x, y, core), basis: 4 (over z).
Axes of the slice: x: 4, y: 4, z: 4, core: 2. Of those that a mesh axis runs over, the one named last changes fastest.
Arguments:
- dist: float32 [32, 4096], P(None, 'struct'), may hold values from 0.8 to 4.8
- nbr_species: int32 [32, 4096], P(None, 'struct'), may hold values from 0 to 8
- species: int32 [4096], P('struct'), may hold values from 0 to 7
- counts: int32 [256], P('struct'), may hold values from 4 to 16
- pattern: int32 [8, 8], replicated, may hold values 0 or 1
- projections: bfloat16 [4, 64, 100352], P(None, None, 'basis'), may hold values from -0.75 to 0.75
- energies: float32 [256], P('struct'), may hold values from -6 to 6
Outputs:
- coefficients: float32 [100352], P('basis')
- row_direction: float32 [256], P('struct')
The draws below stay inside these ranges and needn't reach their ends.
Inputs may be any that keep to these rules, and one draw needn't show every extreme that they name: `nbr_species`: the value 8 marks an empty neighbour slot.
All inputs are finite; a program needn't handle non-finite values.
Results may differ from the reference program's by a relative error of at most 0.0003.
The reference program's roundings to bfloat16 on the way (of `atomic`) count: a program that leaves them out, or rounds other values in their place, can miss the bound.
Values may be sent and summed in bfloat16 or wider, within the bound.
No kernel may reach another device: no remote copies, remote signals or barrier semaphores. Data moves between devices by JAX's collectives and lax.ppermute only.
A program may use at most 128 MiB of HBM per device.

```python
import math
import jax
import jax.numpy as jnp
import numpy as np
from jax import lax

SPECIES = 8
RADIAL = 8
FACTORS = 4
K_SPEC = 12544
MAXAT = 16
NB = 32
ITERS = 4
C = 64
K = 100352
STRUCTS = 256
ATOMS = 4096


def set_ends(result, own_key, low, top_value):
    index_at = [jax.random.randint(jax.random.fold_in(own_key, axis), (), 0, length) for axis, length in enumerate(result.shape)]
    widest = result.shape.index(max(result.shape))
    beside = index_at[:widest] + [(index_at[widest] + 1) % result.shape[widest]] + index_at[widest + 1:]
    return result.at[tuple(index_at)].set(low).at[tuple(beside)].set(top_value)


def level_of(stream_key, dims, pieces, low, top_value):
    factor_of = 1.0
    for position, shards_of in pieces:
        draws = jax.random.uniform(jax.random.fold_in(jax.random.fold_in(stream_key, 6), position), (shards_of,), jnp.float32, low / len(pieces), top_value / len(pieces))
        factor_of = factor_of * jnp.repeat(jnp.exp(draws), dims[position] // shards_of).reshape((-1,) + (1,) * (len(dims) - 1 - position))
    return factor_of


def rank_table(amount, lean):
    weights = [(1 << 20) // math.isqrt(standing ** lean) + 1 for standing in range(1, amount + 1)]
    width = 1 + sum(weights) // (1 << 30)
    return np.cumsum(np.array([max(1, weight // width) for weight in weights]))


def ranked_ids(key, dims, amount, slope):
    grid = rank_table(amount, slope)
    pick = jax.random.randint(jax.random.fold_in(key, 1), dims, 0, int(grid[amount - 1]))
    standing = jnp.searchsorted(jnp.asarray(grid, jnp.int32), pick, side="right")
    return jax.random.permutation(jax.random.fold_in(key, 2), amount)[standing].astype(jnp.int32)


def centred(own_key, shape, scale, most, cuts=(), kind=jnp.bfloat16):
    result = jax.random.normal(own_key, shape, jnp.float32) * scale
    if len(cuts) > 0:
        result = level_of(own_key, shape, cuts, -0.22, 0.18) * result
    return jnp.clip(result, min=-most, max=most).astype(kind)


def setup_inputs(seed: int = 0) -> dict:
    streams_of = jax.random.split(jax.random.key(seed), 8)
    return {
        "dist": jnp.clip(0.8 + 4 * jax.random.uniform(streams_of[0], (NB, ATOMS), jnp.float32) ** level_of(streams_of[0], (NB, ATOMS), ((1, 32),), -0.2, 0.2), 0.8, 4.8),
        "nbr_species": set_ends(jax.random.randint(streams_of[1], (NB, ATOMS), 0, SPECIES + 1), jax.random.fold_in(streams_of[1], 1), 0, SPECIES).astype(jnp.int32),
        "species": set_ends(ranked_ids(streams_of[2], (ATOMS,), SPECIES, 2), jax.random.fold_in(streams_of[2], 3), 0, SPECIES - 1).astype(jnp.int32),
        "counts": set_ends(jax.random.randint(streams_of[3], (STRUCTS,), max(1, MAXAT // 4), MAXAT + 1), jax.random.fold_in(streams_of[3], 1), max(1, MAXAT // 4), MAXAT).astype(jnp.int32),
        "pattern": set_ends((jax.random.randint(streams_of[4], (SPECIES, SPECIES), 0, 4) < 3).astype(jnp.int32), jax.random.fold_in(streams_of[4], 1), 0, 1),
        "projections": centred(streams_of[5], (FACTORS, C, K), C ** -0.5, 0.75, ((2, 4),)),
        "energies": centred(streams_of[6], (STRUCTS,), 1.0, 6.0, ((0, 32),), jnp.float32),
    }


HIGH = lax.Precision.HIGHEST
CUTOFF = 5.0

def atomic_basis(dist, nbr_species, species, counts, pattern):
    kinds = jnp.arange(SPECIES, dtype=jnp.int32)
    ratio = dist / CUTOFF
    envelope = (1.0 - ratio) * (1.0 - ratio)
    orders = jnp.arange(RADIAL, dtype=jnp.int32).astype(jnp.float32)
    radial = envelope[None] * jnp.cos(jnp.pi * orders[:, None, None] * ratio[None])
    center = (species[None, :] == kinds[:, None]).astype(jnp.float32)
    allowed = jnp.dot(pattern.astype(jnp.float32).T, center, precision=HIGH)
    match = (nbr_species[None] == kinds[:, None, None]).astype(jnp.float32) * allowed[:, None, :]
    atomic = jnp.einsum('ena,rna->aer', match, radial, precision=HIGH)
    atomic = atomic.reshape(atomic.shape[0], SPECIES * RADIAL).astype(jnp.bfloat16)
    slots = jnp.arange(species.shape[0], dtype=jnp.int32) % MAXAT
    per_atom = jnp.repeat(counts, MAXAT)
    weight = jnp.where(slots < per_atom, 1.0 / per_atom.astype(jnp.float32), jnp.float32(0.0))
    return (atomic, weight.astype(jnp.float32))

def design_rows(atomic, weight, species, projections):

    def block(element):
        columns = lax.dynamic_slice_in_dim(projections, element * K_SPEC, K_SPEC, 2)
        product = jnp.dot(atomic, columns[0], preferred_element_type=jnp.float32)
        for factor in range(1, FACTORS):
            product = product * jnp.dot(atomic, columns[factor], preferred_element_type=jnp.float32)
        scale = jnp.where(species == element, weight, jnp.float32(0.0))
        terms = product * scale[:, None]
        return terms.reshape(-1, MAXAT, K_SPEC).sum(axis=1)
    rows = lax.map(block, jnp.arange(SPECIES, dtype=jnp.int32))
    return jnp.transpose(rows, (1, 0, 2)).reshape(rows.shape[1], SPECIES * K_SPEC)

def reference(dist, nbr_species, species, counts, pattern, projections, energies):
    atomic, weight = atomic_basis(dist, nbr_species, species, counts, pattern)
    design = design_rows(atomic, weight, species, projections)
    beta = jnp.sqrt(jnp.sum(energies * energies))
    left = energies / beta
    right = jnp.dot(left, design, precision=HIGH)
    alpha = jnp.sqrt(jnp.sum(right * right))
    right = right / alpha
    search = right
    iterate = jnp.zeros_like(right)
    phibar = beta
    rhobar = alpha
    for step_index in range(ITERS):
        left = jnp.dot(design, right, precision=HIGH) - alpha * left
        beta = jnp.sqrt(jnp.sum(left * left))
        left = left / beta
        right = jnp.dot(left, design, precision=HIGH) - beta * right
        alpha = jnp.sqrt(jnp.sum(right * right))
        right = right / alpha
        rho = jnp.sqrt(rhobar * rhobar + beta * beta)
        cosine = rhobar / rho
        sine = beta / rho
        theta = sine * alpha
        rhobar = -cosine * alpha
        advance = cosine * phibar
        phibar = sine * phibar
        iterate = iterate + advance / rho * search
        search = right - theta / rho * search
    total = jnp.sum(iterate * iterate)
    coefficients = iterate * (jnp.sqrt(jnp.float32(K)) / jnp.sqrt(total))
    row_direction = left * jnp.sqrt(jnp.float32(STRUCTS))
    return (coefficients, row_direction)
```

```python
import functools
import math

import jax
import jax.numpy as jnp
from jax import lax
from jax.experimental import pallas as pl
from jax.experimental.pallas import tpu as pltpu
from jax.sharding import Mesh, PartitionSpec as P

SPECIES = 8
RADIAL = 8
FACTORS = 4
CHANNELS = 64
K_SPEC = 12544
MAXAT = 16
ITERS = 4
K = 100352
STRUCTS = 256

LANES = 128
WIDTH = 896
PER_SPEC = K_SPEC // WIDTH
LOCAL = 8
BLOCK = LOCAL * MAXAT
PACKED = 72
CODE, COUNT, ENERGY = 64, 65, 66
GROUP = 32

STRUCT = ("chip", "core")
CUTOFF = 5.0
PI_HIGH = 3.140625
PI_MID = 0.0009670257568359375
PI_LOW = math.pi - PI_HIGH - PI_MID
COS_TERMS = tuple((-1.0) ** n / math.factorial(2 * n) for n in range(9))


def cosine(angle):
    turns = jnp.floor(angle * (1.0 / math.pi) + 0.5)
    rest = angle - turns * PI_HIGH
    rest = rest - turns * PI_MID
    rest = rest - turns * PI_LOW
    square = rest * rest
    value = jnp.full_like(square, COS_TERMS[-1])
    for term in COS_TERMS[-2::-1]:
        value = value * square + term
    odd = turns - 2.0 * jnp.floor(turns * 0.5)
    return value * (1.0 - 2.0 * odd)


def atomic_kernel(dist_ref, nbr_ref, species_ref, counts_ref, pattern_ref, energies_ref, out_ref):
    ratio = dist_ref[...] / CUTOFF
    envelope = (1.0 - ratio) * (1.0 - ratio)
    nbr = nbr_ref[...]
    species = species_ref[...]
    radial = []
    for order in range(RADIAL):
        if order == 0:
            radial.append(envelope)
        else:
            radial.append(envelope * cosine((jnp.float32(math.pi) * jnp.float32(order)) * ratio))
    rows = []
    for element in range(SPECIES):
        allowed = jnp.zeros(species.shape, jnp.float32)
        for center in range(SPECIES):
            seen = pattern_ref[center, element].astype(jnp.float32)
            allowed = jnp.where(species == center, seen, allowed)
        match = jnp.where(nbr == element, allowed, 0.0)
        for order in range(RADIAL):
            rows.append(jnp.sum(match * radial[order], axis=0, keepdims=True))
    atomic = jnp.concatenate(rows, axis=0).astype(jnp.bfloat16)

    lane = lax.broadcasted_iota(jnp.int32, (1, LANES), 1)
    slots = lane % MAXAT
    per_atom = jnp.zeros((1, LANES), jnp.int32)
    count = jnp.zeros((1, LANES), jnp.float32)
    energy = jnp.zeros((1, LANES), jnp.float32)
    for structure in range(LOCAL):
        amount = counts_ref[structure]
        per_atom = jnp.where(lane // MAXAT == structure, amount, per_atom)
        count = jnp.where(lane == structure, amount.astype(jnp.float32), count)
        energy = jnp.where(lane == structure, energies_ref[structure], energy)
    code = jnp.where(slots < per_atom, species, SPECIES).astype(jnp.float32)
    parts = [code, count]
    for _ in range(3):
        part = energy.astype(jnp.bfloat16).astype(jnp.float32)
        parts.append(part)
        energy = energy - part
    parts.append(jnp.zeros((PACKED - CHANNELS - len(parts), LANES), jnp.float32))
    packed = jnp.concatenate([atomic, jnp.concatenate(parts, axis=0).astype(jnp.bfloat16)], axis=0)
    for copy in range(out_ref.shape[0]):
        out_ref[copy, :, :] = packed


def atomic_call(dist, nbr_species, species, counts, pattern, energies, copies):
    vmem = pl.BlockSpec(memory_space=pltpu.VMEM)
    smem = pl.BlockSpec(memory_space=pltpu.SMEM)
    return pl.pallas_call(
        atomic_kernel,
        out_shape=jax.ShapeDtypeStruct((copies, PACKED, LANES), jnp.bfloat16),
        in_specs=[vmem, vmem, vmem, smem, smem, smem],
        out_specs=vmem,
        name="atomic",
    )(dist, nbr_species, species.reshape(1, -1), counts, pattern, energies)


def maps_kernel(maps_ref, out_ref):
    for left in range(0, WIDTH, LANES):
        for factor in range(FACTORS):
            turned = maps_ref[factor, :, left : left + LANES].astype(jnp.float32).T.astype(jnp.bfloat16)
            for half in range(LANES // GROUP):
                row = ((left // GROUP + half) * FACTORS + factor) * GROUP
                out_ref[row : row + GROUP, :] = turned[half * GROUP : (half + 1) * GROUP]


def maps_call(maps):
    vmem = pl.BlockSpec(memory_space=pltpu.VMEM)
    return pl.pallas_call(
        maps_kernel,
        out_shape=jax.ShapeDtypeStruct((FACTORS * WIDTH, CHANNELS), jnp.bfloat16),
        in_specs=[vmem],
        out_specs=vmem,
        compiler_params=pltpu.CompilerParams(vmem_limit_bytes=8 * 1024 * 1024),
        cost_estimate=pl.CostEstimate(flops=0, bytes_accessed=1400000, transcendentals=0),
        name="maps",
    )(maps)


def upto_each(element, atoms_ref):
    codes = atoms_ref[:, CODE, :].astype(jnp.float32)
    lane = lax.broadcasted_iota(jnp.int32, codes.shape, 1)
    chosen = jnp.where(codes == element, 1.0, 0.0)
    upto = chosen
    for reach in (1, 2, 4, 8):
        upto = upto + jnp.where(lane % MAXAT >= reach, pltpu.roll(upto, reach, 1), 0.0)
    return chosen, upto


def move_atoms(chosen, upto, atoms_ref, ranked_ref):
    structure = lax.broadcasted_iota(jnp.int32, chosen.shape, 1) // MAXAT
    target = jnp.where(chosen > 0.0, (upto - 1.0) * LOCAL + structure.astype(jnp.float32), -1.0).astype(jnp.bfloat16)
    rows = lax.broadcasted_iota(jnp.int32, (BLOCK, LANES), 0).astype(jnp.float32).astype(jnp.bfloat16)
    one, zero = jnp.ones(rows.shape, jnp.bfloat16), jnp.zeros(rows.shape, jnp.bfloat16)
    for chip in range(atoms_ref.shape[0]):
        move = jnp.where(jnp.broadcast_to(target[chip : chip + 1, :], rows.shape) == rows, one, zero)
        moved = lax.dot_general(
            move, atoms_ref[chip, :CHANNELS, :], (((1,), (1,)), ((), ())), preferred_element_type=jnp.float32
        )
        for rank in range(MAXAT):
            ranked_ref[rank, chip * LOCAL : (chip + 1) * LOCAL, :] = moved[rank * LOCAL : (rank + 1) * LOCAL]


def ranked_kernel(where_ref, own_ref, ranked_ref):
    move_atoms(*upto_each(where_ref[0].astype(jnp.float32), own_ref), own_ref, ranked_ref)


def ranked_call(where, own):
    vmem = pl.BlockSpec(memory_space=pltpu.VMEM)
    return pl.pallas_call(
        ranked_kernel,
        out_shape=jax.ShapeDtypeStruct((MAXAT, own.shape[0] * LOCAL, CHANNELS), jnp.float32),
        in_specs=[pl.BlockSpec(memory_space=pltpu.SMEM), vmem],
        out_specs=vmem,
        compiler_params=pltpu.CompilerParams(vmem_limit_bytes=8 * 1024 * 1024),
        cost_estimate=pl.CostEstimate(flops=40000000, bytes_accessed=1400000, transcendentals=0),
        name="ranked",
    )(where, own)


def design_kernel(where_ref, own_ref, other_ref, first_ref, maps_ref, high_ref, low_ref, gram_ref, second_ref, design_ref):
    element = where_ref[0].astype(jnp.float32)
    core = where_ref[2]
    chosen, upto = upto_each(element, other_ref)
    ranks = jnp.max(jnp.maximum(upto, upto_each(element, own_ref)[1])).astype(jnp.int32)
    move_atoms(chosen, upto, other_ref, second_ref)
    over = (((1,), (1,)), ((), ()))
    design_ref[...] = jnp.zeros(design_ref.shape, jnp.float32)

    def terms(atoms, left):
        columns = maps_ref[left * FACTORS : (left + GROUP) * FACTORS, :]
        values = lax.dot_general(columns, atoms, over, preferred_element_type=jnp.float32)
        product = values[:GROUP]
        for factor in range(1, FACTORS):
            product = product * values[factor * GROUP : (factor + 1) * GROUP]
        return product

    def add_ranks(first, amount):
        atoms = []
        for rank in range(amount):
            own, other = first_ref[first + rank], second_ref[first + rank]
            halves = [jnp.where(core == 0, own, other), jnp.where(core == 0, other, own)]
            atoms.append(jnp.concatenate(halves, axis=0).astype(jnp.bfloat16))
        for left in range(0, WIDTH, GROUP):
            design_ref[left : left + GROUP, :] += sum(terms(operand, left) for operand in atoms)

    def add_fours(turn, carry):
        add_ranks(turn * 4, 4)
        return carry

    lax.fori_loop(0, ranks // 4, add_fours, 0)

    @pl.when(ranks % 4 >= 2)
    def _():
        add_ranks(ranks // 4 * 4, 2)

    @pl.when(ranks % 2 == 1)
    def _():
        add_ranks(ranks - 1, 1)

    design = design_ref[...]
    high = design.astype(jnp.bfloat16)
    low = (design - high.astype(jnp.float32)).astype(jnp.bfloat16)
    high_ref[...] = high
    low_ref[...] = low
    down = (((0,), (0,)), ((), ()))
    gram = lax.dot_general(high, high, down, preferred_element_type=jnp.float32)
    gram += lax.dot_general(high, low, down, preferred_element_type=jnp.float32)
    gram += lax.dot_general(low, high, down, preferred_element_type=jnp.float32)
    for left in range(0, STRUCTS, LANES):
        gram_ref[left // LANES * STRUCTS : (left // LANES + 1) * STRUCTS, :] = gram[:, left : left + LANES]


def design_call(where, own, other, ranked, maps):
    vmem = pl.BlockSpec(memory_space=pltpu.VMEM)
    return pl.pallas_call(
        design_kernel,
        out_shape=(
            jax.ShapeDtypeStruct((WIDTH, STRUCTS), jnp.bfloat16),
            jax.ShapeDtypeStruct((WIDTH, STRUCTS), jnp.bfloat16),
            jax.ShapeDtypeStruct((STRUCTS * STRUCTS // LANES, LANES), jnp.float32),
        ),
        in_specs=[pl.BlockSpec(memory_space=pltpu.SMEM)] + [vmem] * 4,
        out_specs=(vmem, vmem, vmem),
        scratch_shapes=[
            pltpu.VMEM((MAXAT, STRUCTS // 2, CHANNELS), jnp.float32),
            pltpu.VMEM((WIDTH, STRUCTS), jnp.float32),
        ],
        compiler_params=pltpu.CompilerParams(vmem_limit_bytes=24 * 1024 * 1024),
        name="design",
    )(where, own, other, ranked, maps)


def total_kernel(parts_ref, out_ref):
    parts = parts_ref[...]
    out_ref[...] = jnp.broadcast_to(jnp.sum(parts, axis=0, keepdims=True), parts.shape)


def total_call(parts):
    vmem = pl.BlockSpec(memory_space=pltpu.VMEM)
    return pl.pallas_call(
        total_kernel,
        out_shape=jax.ShapeDtypeStruct(parts.shape, parts.dtype),
        in_specs=[vmem],
        out_specs=vmem,
        compiler_params=pltpu.CompilerParams(vmem_limit_bytes=4 * 1024 * 1024),
        name="total",
    )(parts)


def split(value, amount):
    parts = []
    for _ in range(amount):
        part = value.astype(jnp.bfloat16)
        parts.append(part)
        value = value - part.astype(jnp.float32)
    return parts


def stacked(vector):
    first, second, third = [part.astype(jnp.float32) for part in split(vector, 3)]
    row = lax.broadcasted_iota(jnp.int32, (16, vector.shape[1]), 0)
    one = jnp.where(row == 0, first, 0.0)
    two = jnp.where(row == 1, second, one)
    three = jnp.where(row == 2, third, two)
    return [operand.astype(jnp.bfloat16) for operand in (three, two)]


def picked(own_ref, other_ref, core):
    chips = own_ref.shape[0]
    kinds = (COUNT, ENERGY, ENERGY + 1, ENERGY + 2)
    parts = [half[:, kind, :].astype(jnp.float32) for kind in kinds for half in (own_ref, other_ref)]
    parts = jnp.concatenate(parts, axis=0).astype(jnp.bfloat16)
    structure = lax.broadcasted_iota(jnp.int32, (LANES, STRUCTS), 1)
    repeat = structure % LOCAL == lax.broadcasted_iota(jnp.int32, (LANES, STRUCTS), 0)
    parts = jnp.dot(parts, jnp.where(repeat, 1.0, 0.0).astype(jnp.bfloat16), preferred_element_type=jnp.float32)
    block = lax.broadcasted_iota(jnp.int32, (2 * chips, STRUCTS), 0)
    block = block % chips + jnp.where(block < chips, core, 1 - core) * chips
    here = block == lax.broadcasted_iota(jnp.int32, (2 * chips, STRUCTS), 1) // LOCAL
    rows = [
        jnp.sum(jnp.where(here, parts[kind * 2 * chips : (kind + 1) * 2 * chips], 0.0), axis=0, keepdims=True)
        for kind in range(len(kinds))
    ]
    return rows[0], rows[1] + rows[2] + rows[3]


def solve_kernel(where_ref, gram_ref, own_ref, other_ref, high_ref, low_ref, coefficients_ref, direction_ref):
    counts, energies = picked(own_ref, other_ref, where_ref[2])
    inverse = 1.0 / counts
    gram = split(jnp.concatenate([gram_ref[:STRUCTS, :], gram_ref[STRUCTS:, :]], axis=1), 2)

    def dot(a, b):
        return jnp.sum(a * b, axis=1, keepdims=True)

    def apply(vector):
        image = jnp.zeros((16, STRUCTS), jnp.float32)
        for operand, part in zip(stacked(vector * inverse), gram):
            image = image + jnp.dot(operand, part, preferred_element_type=jnp.float32)
        return jnp.sum(image, axis=0, keepdims=True) * inverse

    image = apply(energies)
    square = dot(energies, energies)
    shrink = lax.rsqrt(square)
    beta = square * shrink
    left = energies * shrink
    right = left
    image = image * shrink
    square = dot(right, image)
    shrink = lax.rsqrt(square)
    alpha = square * shrink
    right, image = right * shrink, image * shrink
    search, search_image = right, image
    iterate = jnp.zeros_like(right)
    iterate_image = iterate
    phibar = beta
    rhobar = alpha
    for step in range(ITERS):
        left = image - alpha * left
        left_image = apply(left) if step < ITERS - 1 else None
        square = dot(left, left)
        shrink = lax.rsqrt(square)
        beta = square * shrink
        left = left * shrink
        over_rho = lax.rsqrt(rhobar * rhobar + square)
        cosine_part = rhobar * over_rho
        sine_part = beta * over_rho
        advance = cosine_part * phibar * over_rho
        phibar = sine_part * phibar
        iterate = iterate + advance * search
        iterate_image = iterate_image + advance * search_image
        if step < ITERS - 1:
            right = left - beta * right
            image = left_image * shrink - beta * image
            square = dot(right, image)
            shrink = lax.rsqrt(square)
            alpha = square * shrink
            right, image = right * shrink, image * shrink
            turn = sine_part * alpha * over_rho
            rhobar = -cosine_part * alpha
            search = right - turn * search
            search_image = image - turn * search_image
    iterate = iterate * (math.sqrt(K) * lax.rsqrt(dot(iterate, iterate_image))) * inverse
    over = (((1,), (1,)), ((), ()))
    values = jnp.zeros((16, WIDTH), jnp.float32)
    for operand, part in zip(stacked(iterate), (high_ref[...], low_ref[...])):
        values = values + lax.dot_general(operand, part, over, preferred_element_type=jnp.float32)
    values = jnp.sum(values, axis=0, keepdims=True)
    rows = jnp.concatenate([values[:, at : at + LANES] for at in range(0, WIDTH, LANES)], axis=0)
    for copy in range(coefficients_ref.shape[0]):
        coefficients_ref[copy] = rows
    direction = jnp.broadcast_to(left * math.sqrt(STRUCTS), (8, STRUCTS))
    direction_ref[...] = pltpu.roll(direction, STRUCTS - where_ref[1] * LOCAL, 1)[:1, :LOCAL]


def solve_call(where, gram, own, other, high, low, copies):
    vmem = pl.BlockSpec(memory_space=pltpu.VMEM)
    return pl.pallas_call(
        solve_kernel,
        out_shape=(
            jax.ShapeDtypeStruct((copies, WIDTH // LANES, LANES), jnp.float32),
            jax.ShapeDtypeStruct((1, LOCAL), jnp.float32),
        ),
        in_specs=[pl.BlockSpec(memory_space=pltpu.SMEM)] + [vmem] * 5,
        out_specs=(vmem, vmem),
        compiler_params=pltpu.CompilerParams(vmem_limit_bytes=16 * 1024 * 1024),
        name="solve",
    )(where, gram, own, other, high, low)


def swap(value):
    return lax.ppermute(value, "core", [(0, 1), (1, 0)])


def body(dist, nbr_species, species, counts, pattern, projections, energies):
    struct = lax.axis_index(STRUCT)
    basis = lax.axis_index("basis")
    structs = lax.axis_size(STRUCT)
    k_local = projections.shape[2]
    owners = k_local // WIDTH
    mine = jnp.minimum(struct, owners - 1)
    element = jnp.where(struct < owners, (basis * owners + struct) // PER_SPEC, SPECIES + 1)
    core, chips = lax.axis_index("core"), lax.axis_size("chip")
    where = jnp.stack([element, core * chips + lax.axis_index("chip"), core]).astype(jnp.int32)

    packed = atomic_call(dist, nbr_species, species, counts, pattern, energies, chips)
    own = lax.all_to_all(packed, "chip", 0, 0)
    maps = maps_call(lax.dynamic_slice_in_dim(projections, mine * WIDTH, WIDTH, 2))
    own, maps, where = lax.optimization_barrier((own, maps, where))
    other = swap(own)
    ranked = ranked_call(where, own)
    high, low, gram = design_call(where, own, other, ranked, maps)
    everyone = ("chip", "core", "basis")
    parts = lax.all_to_all(gram.reshape(lax.axis_size(everyone), -1, LANES), everyone, 0, 0)
    gram = lax.all_to_all(total_call(parts), everyone, 0, 0).reshape(-1, LANES)
    values, direction = solve_call(where, gram, own, other, high, low, structs)
    values = lax.all_to_all(values, STRUCT, 0, 0)
    return (values[:owners].reshape(-1), direction.reshape(-1))


def solution(mesh):
    chips = Mesh(mesh.devices.reshape(-1, 2, mesh.shape["basis"]), ("chip", "core", "basis"))
    placed = (
        P(None, STRUCT),
        P(None, STRUCT),
        P(STRUCT),
        P(STRUCT),
        P(),
        P(None, None, "basis"),
        P(STRUCT),
    )
    return jax.shard_map(
        body, mesh=chips, in_specs=placed, out_specs=(P("basis"), P(STRUCT)), check_vma=False
    )
```

```python
import functools
import math

import jax
import jax.numpy as jnp
from jax import lax
from jax.experimental import pallas as pl
from jax.experimental.pallas import tpu as pltpu
from jax.sharding import Mesh, PartitionSpec as P

SPECIES = 8
RADIAL = 8
FACTORS = 4
CHANNELS = 64
K_SPEC = 12544
MAXAT = 16
ITERS = 4
K = 100352
STRUCTS = 256

LANES = 128
WIDTH = 896
PER_SPEC = K_SPEC // WIDTH
LOCAL = 8
BLOCK = LOCAL * MAXAT
PACKED = 72
CODE, COUNT, ENERGY = 64, 65, 66
GROUP = 32

STRUCT = ("chip", "core")
CUTOFF = 5.0
PI_HIGH = 3.140625
PI_MID = 0.0009670257568359375
PI_LOW = math.pi - PI_HIGH - PI_MID
COS_TERMS = tuple((-1.0) ** n / math.factorial(2 * n) for n in range(9))


def cosine(angle):
    turns = jnp.floor(angle * (1.0 / math.pi) + 0.5)
    rest = angle - turns * PI_HIGH
    rest = rest - turns * PI_MID
    rest = rest - turns * PI_LOW
    square = rest * rest
    value = jnp.full_like(square, COS_TERMS[-1])
    for term in COS_TERMS[-2::-1]:
        value = value * square + term
    odd = turns - 2.0 * jnp.floor(turns * 0.5)
    return value * (1.0 - 2.0 * odd)


def atomic_kernel(dist_ref, nbr_ref, species_ref, counts_ref, pattern_ref, energies_ref, out_ref):
    ratio = dist_ref[...] / CUTOFF
    envelope = (1.0 - ratio) * (1.0 - ratio)
    nbr = nbr_ref[...]
    species = species_ref[...]
    radial = []
    for order in range(RADIAL):
        if order == 0:
            radial.append(envelope)
        else:
            radial.append(envelope * cosine((jnp.float32(math.pi) * jnp.float32(order)) * ratio))
    rows = []
    for element in range(SPECIES):
        allowed = jnp.zeros(species.shape, jnp.float32)
        for center in range(SPECIES):
            seen = pattern_ref[center, element].astype(jnp.float32)
            allowed = jnp.where(species == center, seen, allowed)
        match = jnp.where(nbr == element, allowed, 0.0)
        for order in range(RADIAL):
            rows.append(jnp.sum(match * radial[order], axis=0, keepdims=True))
    atomic = jnp.concatenate(rows, axis=0).astype(jnp.bfloat16)

    lane = lax.broadcasted_iota(jnp.int32, (1, LANES), 1)
    slots = lane % MAXAT
    per_atom = jnp.zeros((1, LANES), jnp.int32)
    count = jnp.zeros((1, LANES), jnp.float32)
    energy = jnp.zeros((1, LANES), jnp.float32)
    for structure in range(LOCAL):
        amount = counts_ref[structure]
        per_atom = jnp.where(lane // MAXAT == structure, amount, per_atom)
        count = jnp.where(lane == structure, amount.astype(jnp.float32), count)
        energy = jnp.where(lane == structure, energies_ref[structure], energy)
    code = jnp.where(slots < per_atom, species, SPECIES).astype(jnp.float32)
    parts = [code, count]
    for _ in range(3):
        part = energy.astype(jnp.bfloat16).astype(jnp.float32)
        parts.append(part)
        energy = energy - part
    parts.append(jnp.zeros((PACKED - CHANNELS - len(parts), LANES), jnp.float32))
    packed = jnp.concatenate([atomic, jnp.concatenate(parts, axis=0).astype(jnp.bfloat16)], axis=0)
    for copy in range(out_ref.shape[0]):
        out_ref[copy, :, :] = packed


def atomic_call(dist, nbr_species, species, counts, pattern, energies, copies):
    vmem = pl.BlockSpec(memory_space=pltpu.VMEM)
    smem = pl.BlockSpec(memory_space=pltpu.SMEM)
    return pl.pallas_call(
        atomic_kernel,
        out_shape=jax.ShapeDtypeStruct((copies, PACKED, LANES), jnp.bfloat16),
        in_specs=[vmem, vmem, vmem, smem, smem, smem],
        out_specs=vmem,
        name="atomic",
    )(dist, nbr_species, species.reshape(1, -1), counts, pattern, energies)


def maps_kernel(maps_ref, out_ref):
    for left in range(0, WIDTH, LANES):
        for factor in range(FACTORS):
            turned = maps_ref[factor, :, left : left + LANES].astype(jnp.float32).T.astype(jnp.bfloat16)
            for half in range(LANES // GROUP):
                row = ((left // GROUP + half) * FACTORS + factor) * GROUP
                out_ref[row : row + GROUP, :] = turned[half * GROUP : (half + 1) * GROUP]


def maps_call(maps):
    vmem = pl.BlockSpec(memory_space=pltpu.VMEM)
    return pl.pallas_call(
        maps_kernel,
        out_shape=jax.ShapeDtypeStruct((FACTORS * WIDTH, CHANNELS), jnp.bfloat16),
        in_specs=[vmem],
        out_specs=vmem,
        compiler_params=pltpu.CompilerParams(vmem_limit_bytes=8 * 1024 * 1024),
        cost_estimate=pl.CostEstimate(flops=0, bytes_accessed=1400000, transcendentals=0),
        name="maps",
    )(maps)


def place():
    core, chips = lax.axis_index("core"), lax.axis_size("chip")
    struct = lax.axis_index("chip") * 2 + core
    owners = SPECIES // lax.axis_size("basis") * PER_SPEC
    element = lax.div(lax.axis_index("basis") * owners + struct, PER_SPEC)
    return core, core * chips + lax.axis_index("chip"), jnp.where(struct < owners, element, SPECIES + 1)


def upto_each(element, atoms_ref):
    codes = atoms_ref[:, CODE, :].astype(jnp.float32)
    lane = lax.broadcasted_iota(jnp.int32, codes.shape, 1)
    chosen = jnp.where(codes == element, 1.0, 0.0)
    upto = chosen
    for reach in (1, 2, 4, 8):
        upto = upto + jnp.where(lane % MAXAT >= reach, pltpu.roll(upto, reach, 1), 0.0)
    return chosen, upto


def move_atoms(chosen, upto, atoms_ref, ranked_ref):
    structure = lax.broadcasted_iota(jnp.int32, chosen.shape, 1) // MAXAT
    target = jnp.where(chosen > 0.0, (upto - 1.0) * LOCAL + structure.astype(jnp.float32), -1.0).astype(jnp.bfloat16)
    rows = lax.broadcasted_iota(jnp.int32, (BLOCK, LANES), 0).astype(jnp.float32).astype(jnp.bfloat16)
    one, zero = jnp.ones(rows.shape, jnp.bfloat16), jnp.zeros(rows.shape, jnp.bfloat16)
    for chip in range(atoms_ref.shape[0]):
        move = jnp.where(jnp.broadcast_to(target[chip : chip + 1, :], rows.shape) == rows, one, zero)
        moved = lax.dot_general(
            move, atoms_ref[chip, :CHANNELS, :], (((1,), (1,)), ((), ())), preferred_element_type=jnp.float32
        )
        for rank in range(MAXAT):
            ranked_ref[rank, chip * LOCAL : (chip + 1) * LOCAL, :] = moved[rank * LOCAL : (rank + 1) * LOCAL]


def ranked_kernel(own_ref, ranked_ref):
    move_atoms(*upto_each(place()[2].astype(jnp.float32), own_ref), own_ref, ranked_ref)


def ranked_call(own):
    vmem = pl.BlockSpec(memory_space=pltpu.VMEM)
    return pl.pallas_call(
        ranked_kernel,
        out_shape=jax.ShapeDtypeStruct((MAXAT, own.shape[0] * LOCAL, CHANNELS), jnp.float32),
        in_specs=[vmem],
        out_specs=vmem,
        compiler_params=pltpu.CompilerParams(vmem_limit_bytes=8 * 1024 * 1024),
        cost_estimate=pl.CostEstimate(flops=40000000, bytes_accessed=1400000, transcendentals=0),
        name="ranked",
    )(own)


def design_kernel(own_ref, other_ref, first_ref, maps_ref, high_ref, low_ref, gram_ref, second_ref, design_ref):
    core, _, element = place()
    element = element.astype(jnp.float32)
    chosen, upto = upto_each(element, other_ref)
    ranks = jnp.max(jnp.maximum(upto, upto_each(element, own_ref)[1])).astype(jnp.int32)
    move_atoms(chosen, upto, other_ref, second_ref)
    over = (((1,), (1,)), ((), ()))
    design_ref[...] = jnp.zeros(design_ref.shape, jnp.float32)

    def terms(atoms, left):
        columns = maps_ref[left * FACTORS : (left + GROUP) * FACTORS, :]
        values = lax.dot_general(columns, atoms, over, preferred_element_type=jnp.float32)
        product = values[:GROUP]
        for factor in range(1, FACTORS):
            product = product * values[factor * GROUP : (factor + 1) * GROUP]
        return product

    def add_ranks(first, amount):
        atoms = []
        for rank in range(amount):
            own, other = first_ref[first + rank], second_ref[first + rank]
            halves = [jnp.where(core == 0, own, other), jnp.where(core == 0, other, own)]
            atoms.append(jnp.concatenate(halves, axis=0).astype(jnp.bfloat16))
        for left in range(0, WIDTH, GROUP):
            design_ref[left : left + GROUP, :] += sum(terms(operand, left) for operand in atoms)

    def add_fours(turn, carry):
        add_ranks(turn * 4, 4)
        return carry

    lax.fori_loop(0, ranks // 4, add_fours, 0)

    @pl.when(ranks % 4 >= 2)
    def _():
        add_ranks(ranks // 4 * 4, 2)

    @pl.when(ranks % 2 == 1)
    def _():
        add_ranks(ranks - 1, 1)

    design = design_ref[...]
    high = design.astype(jnp.bfloat16)
    low = (design - high.astype(jnp.float32)).astype(jnp.bfloat16)
    high_ref[...] = high
    low_ref[...] = low
    down = (((0,), (0,)), ((), ()))
    gram = lax.dot_general(high, high, down, preferred_element_type=jnp.float32)
    gram += lax.dot_general(high, low, down, preferred_element_type=jnp.float32)
    gram += lax.dot_general(low, high, down, preferred_element_type=jnp.float32)
    for left in range(0, STRUCTS, LANES):
        gram_ref[left // LANES * STRUCTS : (left // LANES + 1) * STRUCTS, :] = gram[:, left : left + LANES]


def design_call(own, other, ranked, maps):
    vmem = pl.BlockSpec(memory_space=pltpu.VMEM)
    return pl.pallas_call(
        design_kernel,
        out_shape=(
            jax.ShapeDtypeStruct((WIDTH, STRUCTS), jnp.bfloat16),
            jax.ShapeDtypeStruct((WIDTH, STRUCTS), jnp.bfloat16),
            jax.ShapeDtypeStruct((STRUCTS * STRUCTS // LANES, LANES), jnp.float32),
        ),
        in_specs=[vmem] * 4,
        out_specs=(vmem, vmem, vmem),
        scratch_shapes=[
            pltpu.VMEM((MAXAT, STRUCTS // 2, CHANNELS), jnp.float32),
            pltpu.VMEM((WIDTH, STRUCTS), jnp.float32),
        ],
        compiler_params=pltpu.CompilerParams(vmem_limit_bytes=24 * 1024 * 1024),
        name="design",
    )(own, other, ranked, maps)


def total_kernel(parts_ref, out_ref):
    parts = parts_ref[...]
    out_ref[...] = jnp.broadcast_to(jnp.sum(parts, axis=0, keepdims=True), parts.shape)


def total_call(parts):
    vmem = pl.BlockSpec(memory_space=pltpu.VMEM)
    return pl.pallas_call(
        total_kernel,
        out_shape=jax.ShapeDtypeStruct(parts.shape, parts.dtype),
        in_specs=[vmem],
        out_specs=vmem,
        compiler_params=pltpu.CompilerParams(vmem_limit_bytes=4 * 1024 * 1024),
        name="total",
    )(parts)


def split(value, amount):
    parts = []
    for _ in range(amount):
        part = value.astype(jnp.bfloat16)
        parts.append(part)
        value = value - part.astype(jnp.float32)
    return parts


def stacked(vector):
    first, second, third = [part.astype(jnp.float32) for part in split(vector, 3)]
    row = lax.broadcasted_iota(jnp.int32, (16, vector.shape[1]), 0)
    one = jnp.where(row == 0, first, 0.0)
    two = jnp.where(row == 1, second, one)
    three = jnp.where(row == 2, third, two)
    return [operand.astype(jnp.bfloat16) for operand in (three, two)]


def picked(own_ref, other_ref, core):
    chips = own_ref.shape[0]
    kinds = (COUNT, ENERGY, ENERGY + 1, ENERGY + 2)
    parts = [half[:, kind, :].astype(jnp.float32) for kind in kinds for half in (own_ref, other_ref)]
    parts = jnp.concatenate(parts, axis=0).astype(jnp.bfloat16)
    structure = lax.broadcasted_iota(jnp.int32, (LANES, STRUCTS), 1)
    repeat = structure % LOCAL == lax.broadcasted_iota(jnp.int32, (LANES, STRUCTS), 0)
    parts = jnp.dot(parts, jnp.where(repeat, 1.0, 0.0).astype(jnp.bfloat16), preferred_element_type=jnp.float32)
    block = lax.broadcasted_iota(jnp.int32, (2 * chips, STRUCTS), 0)
    block = block % chips + jnp.where(block < chips, core, 1 - core) * chips
    here = block == lax.broadcasted_iota(jnp.int32, (2 * chips, STRUCTS), 1) // LOCAL
    rows = [
        jnp.sum(jnp.where(here, parts[kind * 2 * chips : (kind + 1) * 2 * chips], 0.0), axis=0, keepdims=True)
        for kind in range(len(kinds))
    ]
    return rows[0], rows[1] + rows[2] + rows[3]


def solve_kernel(gram_ref, own_ref, other_ref, high_ref, low_ref, coefficients_ref, direction_ref):
    core, number, _ = place()
    counts, energies = picked(own_ref, other_ref, core)
    inverse = 1.0 / counts
    gram = split(jnp.concatenate([gram_ref[:STRUCTS, :], gram_ref[STRUCTS:, :]], axis=1), 2)

    def dot(a, b):
        return jnp.sum(a * b, axis=1, keepdims=True)

    def apply(vector):
        image = jnp.zeros((16, STRUCTS), jnp.float32)
        for operand, part in zip(stacked(vector * inverse), gram):
            image = image + jnp.dot(operand, part, preferred_element_type=jnp.float32)
        return jnp.sum(image, axis=0, keepdims=True) * inverse

    image = apply(energies)
    square = dot(energies, energies)
    shrink = lax.rsqrt(square)
    beta = square * shrink
    left = energies * shrink
    right = left
    image = image * shrink
    square = dot(right, image)
    shrink = lax.rsqrt(square)
    alpha = square * shrink
    right, image = right * shrink, image * shrink
    search, search_image = right, image
    iterate = jnp.zeros_like(right)
    iterate_image = iterate
    phibar = beta
    rhobar = alpha
    for step in range(ITERS):
        left = image - alpha * left
        left_image = apply(left) if step < ITERS - 1 else None
        square = dot(left, left)
        shrink = lax.rsqrt(square)
        beta = square * shrink
        left = left * shrink
        over_rho = lax.rsqrt(rhobar * rhobar + square)
        cosine_part = rhobar * over_rho
        sine_part = beta * over_rho
        advance = cosine_part * phibar * over_rho
        phibar = sine_part * phibar
        iterate = iterate + advance * search
        iterate_image = iterate_image + advance * search_image
        if step < ITERS - 1:
            right = left - beta * right
            image = left_image * shrink - beta * image
            square = dot(right, image)
            shrink = lax.rsqrt(square)
            alpha = square * shrink
            right, image = right * shrink, image * shrink
            turn = sine_part * alpha * over_rho
            rhobar = -cosine_part * alpha
            search = right - turn * search
            search_image = image - turn * search_image
    iterate = iterate * (math.sqrt(K) * lax.rsqrt(dot(iterate, iterate_image))) * inverse
    over = (((1,), (1,)), ((), ()))
    values = jnp.zeros((16, WIDTH), jnp.float32)
    for operand, part in zip(stacked(iterate), (high_ref[...], low_ref[...])):
        values = values + lax.dot_general(operand, part, over, preferred_element_type=jnp.float32)
    values = jnp.sum(values, axis=0, keepdims=True)
    rows = jnp.concatenate([values[:, at : at + LANES] for at in range(0, WIDTH, LANES)], axis=0)
    for copy in range(coefficients_ref.shape[0]):
        coefficients_ref[copy] = rows
    direction = jnp.broadcast_to(left * math.sqrt(STRUCTS), (8, STRUCTS))
    direction_ref[...] = pltpu.roll(direction, STRUCTS - number * LOCAL, 1)[:1, :LOCAL]


def solve_call(gram, own, other, high, low, copies):
    vmem = pl.BlockSpec(memory_space=pltpu.VMEM)
    return pl.pallas_call(
        solve_kernel,
        out_shape=(
            jax.ShapeDtypeStruct((copies, WIDTH // LANES, LANES), jnp.float32),
            jax.ShapeDtypeStruct((1, LOCAL), jnp.float32),
        ),
        in_specs=[vmem] * 5,
        out_specs=(vmem, vmem),
        compiler_params=pltpu.CompilerParams(vmem_limit_bytes=16 * 1024 * 1024),
        name="solve",
    )(gram, own, other, high, low)


def swap(value):
    return lax.ppermute(value, "core", [(0, 1), (1, 0)])


def body(dist, nbr_species, species, counts, pattern, projections, energies):
    struct = lax.axis_index(STRUCT)
    structs = lax.axis_size(STRUCT)
    owners = projections.shape[2] // WIDTH
    mine = jnp.minimum(struct, owners - 1)

    packed = atomic_call(dist, nbr_species, species, counts, pattern, energies, lax.axis_size("chip"))
    own = lax.all_to_all(packed, "chip", 0, 0)
    maps = maps_call(lax.dynamic_slice_in_dim(projections, mine * WIDTH, WIDTH, 2))
    own, maps = lax.optimization_barrier((own, maps))
    other = swap(own)
    ranked = ranked_call(own)
    high, low, gram = design_call(own, other, ranked, maps)
    everyone = ("chip", "core", "basis")
    parts = lax.all_to_all(gram.reshape(lax.axis_size(everyone), -1, LANES), everyone, 0, 0)
    gram = lax.all_to_all(total_call(parts), everyone, 0, 0).reshape(-1, LANES)
    values, direction = solve_call(gram, own, other, high, low, structs)
    values = lax.all_to_all(values, STRUCT, 0, 0)
    return (values[:owners].reshape(-1), direction.reshape(-1))


def solution(mesh):
    chips = Mesh(mesh.devices.reshape(-1, 2, mesh.shape["basis"]), ("chip", "core", "basis"))
    placed = (
        P(None, STRUCT),
        P(None, STRUCT),
        P(STRUCT),
        P(STRUCT),
        P(),
        P(None, None, "basis"),
        P(STRUCT),
    )
    return jax.shard_map(
        body, mesh=chips, in_specs=placed, out_specs=(P("basis"), P(STRUCT)), check_vma=False
    )
```

```python
import functools
import math

import jax
import jax.numpy as jnp
from jax import lax
from jax.experimental import pallas as pl
from jax.experimental.pallas import tpu as pltpu
from jax.sharding import Mesh, PartitionSpec as P

SPECIES = 8
RADIAL = 8
FACTORS = 4
CHANNELS = 64
K_SPEC = 12544
MAXAT = 16
ITERS = 4
K = 100352
STRUCTS = 256

LANES = 128
WIDTH = 896
PER_SPEC = K_SPEC // WIDTH
LOCAL = 8
BLOCK = LOCAL * MAXAT
PACKED = 72
CODE, COUNT, ENERGY = 64, 65, 66
GROUP = 64
FLAGS = 16

STRUCT = ("chip", "core")
CUTOFF = 5.0
PI_HIGH = 3.140625
PI_MID = 0.0009670257568359375
PI_LOW = math.pi - PI_HIGH - PI_MID
COS_TERMS = tuple((-1.0) ** n / math.factorial(2 * n) for n in range(9))


def cosine(angle):
    turns = jnp.floor(angle * (1.0 / math.pi) + 0.5)
    rest = angle - turns * PI_HIGH
    rest = rest - turns * PI_MID
    rest = rest - turns * PI_LOW
    square = rest * rest
    value = jnp.full_like(square, COS_TERMS[-1])
    for term in COS_TERMS[-2::-1]:
        value = value * square + term
    odd = turns - 2.0 * jnp.floor(turns * 0.5)
    return value * (1.0 - 2.0 * odd)


def atomic_kernel(dist_ref, nbr_ref, species_ref, counts_ref, pattern_ref, energies_ref, out_ref):
    ratio = dist_ref[...] / CUTOFF
    envelope = (1.0 - ratio) * (1.0 - ratio)
    nbr = nbr_ref[...]
    species = species_ref[...]
    radial = []
    for order in range(RADIAL):
        if order == 0:
            radial.append(envelope)
        else:
            radial.append(envelope * cosine((jnp.float32(math.pi) * jnp.float32(order)) * ratio))
    lane = lax.broadcasted_iota(jnp.int32, (SPECIES, LANES), 1)
    row = lax.broadcasted_iota(jnp.int32, (SPECIES, LANES), 0)
    center = jnp.where(species == row, 1.0, 0.0).astype(jnp.bfloat16)
    pattern = pattern_ref[...].astype(jnp.float32).astype(jnp.bfloat16)
    allowed = lax.dot_general(pattern, center, (((0,), (0,)), ((), ())), preferred_element_type=jnp.float32)
    rows = []
    for element in range(SPECIES):
        match = jnp.where(nbr == element, allowed[element : element + 1], 0.0)
        for order in range(RADIAL):
            rows.append(jnp.sum(match * radial[order], axis=0, keepdims=True))
    atomic = jnp.concatenate(rows, axis=0).astype(jnp.bfloat16)

    small = [counts_ref[...].astype(jnp.float32)]
    energy = energies_ref[...]
    for _ in range(3):
        small.append(energy.astype(jnp.bfloat16).astype(jnp.float32))
        energy = energy - small[-1]
    small = jnp.concatenate(small + [jnp.zeros((4, LOCAL), jnp.float32)], axis=0).astype(jnp.bfloat16)
    spots = jnp.concatenate([lane // MAXAT == row, lane == row], axis=1)
    small = jnp.dot(small, jnp.where(spots, 1.0, 0.0).astype(jnp.bfloat16), preferred_element_type=jnp.float32)
    slots = (lane[:1] % MAXAT).astype(jnp.float32)
    code = jnp.where(slots < small[:1, :LANES], species, SPECIES).astype(jnp.float32)
    parts = [code, small[:4, LANES:]]
    parts.append(jnp.zeros((PACKED - CHANNELS - 5, LANES), jnp.float32))
    packed = jnp.concatenate([atomic, jnp.concatenate(parts, axis=0).astype(jnp.bfloat16)], axis=0)
    for copy in range(out_ref.shape[0]):
        out_ref[copy, :, :] = packed


def atomic_call(dist, nbr_species, species, counts, pattern, energies, copies):
    vmem = pl.BlockSpec(memory_space=pltpu.VMEM)
    return pl.pallas_call(
        atomic_kernel,
        out_shape=jax.ShapeDtypeStruct((copies, PACKED, LANES), jnp.bfloat16),
        in_specs=[vmem] * 6,
        out_specs=vmem,
        name="atomic",
    )(dist, nbr_species, species.reshape(1, -1), counts.reshape(1, -1), pattern, energies.reshape(1, -1))


def maps_kernel(maps_ref, out_ref):
    for left in range(0, WIDTH, LANES):
        for factor in range(FACTORS):
            turned = maps_ref[factor, :, left : left + LANES].astype(jnp.float32).T.astype(jnp.bfloat16)
            for half in range(LANES // GROUP):
                row = ((left // GROUP + half) * FACTORS + factor) * GROUP
                out_ref[row : row + GROUP, :] = turned[half * GROUP : (half + 1) * GROUP]


def maps_call(maps):
    vmem = pl.BlockSpec(memory_space=pltpu.VMEM)
    return pl.pallas_call(
        maps_kernel,
        out_shape=jax.ShapeDtypeStruct((FACTORS * WIDTH, CHANNELS), jnp.bfloat16),
        in_specs=[vmem],
        out_specs=vmem,
        compiler_params=pltpu.CompilerParams(vmem_limit_bytes=8 * 1024 * 1024),
        cost_estimate=pl.CostEstimate(flops=0, bytes_accessed=1400000, transcendentals=0),
        name="maps",
    )(maps)


def place():
    core, chips = lax.axis_index("core"), lax.axis_size("chip")
    struct = lax.axis_index("chip") * 2 + core
    owners = SPECIES // lax.axis_size("basis") * PER_SPEC
    element = lax.div(lax.axis_index("basis") * owners + struct, PER_SPEC)
    return core, core * chips + lax.axis_index("chip"), jnp.where(struct < owners, element, SPECIES + 1)


def share_out(element, atoms_ref):
    codes = atoms_ref[:, CODE, :].astype(jnp.float32)
    lane = lax.broadcasted_iota(jnp.int32, codes.shape, 1)
    slot, structure = lane % MAXAT, (lane // MAXAT).astype(jnp.float32)
    chosen = jnp.where(codes == element, 1.0, 0.0)
    upto, since = chosen, chosen
    for reach in (1, 2, 4, 8):
        upto = upto + jnp.where(slot >= reach, pltpu.roll(upto, reach, 1), 0.0)
        since = since + jnp.where(slot < MAXAT - reach, pltpu.roll(since, LANES - reach, 1), 0.0)
    amount = upto + since - chosen
    partner = pltpu.roll(amount, codes.shape[0] // 2, 0)
    held = jnp.floor((amount + partner + 1.0) * 0.5)
    rank = upto - 1.0
    stays = jnp.where((chosen > 0.0) & (rank < held), rank * LOCAL + structure, -1.0)
    leaves = jnp.where((chosen > 0.0) & (rank >= held), (partner + rank - held) * LOCAL + structure, -1.0)
    return stays.astype(jnp.bfloat16), leaves.astype(jnp.bfloat16), held


def move_atoms(stays, leaves, atoms_ref, ranked_ref):
    chips = atoms_ref.shape[0]
    rows = lax.broadcasted_iota(jnp.int32, (BLOCK, LANES), 0).astype(jnp.float32).astype(jnp.bfloat16)
    one, zero = jnp.ones(rows.shape, jnp.bfloat16), jnp.zeros(rows.shape, jnp.bfloat16)
    flags = jnp.concatenate([one[:FLAGS], zero[:FLAGS]], axis=1)

    def hits(target):
        return jnp.where(jnp.broadcast_to(target, rows.shape) == rows, one, zero)

    for chip in range(0, chips, 2):
        pair = []
        for to in (chip, chip + 1):
            source = (to + chips // 2) % chips
            move = jnp.concatenate([hits(stays[to : to + 1, :]), hits(leaves[source : source + 1, :])], axis=1)
            atoms = jnp.concatenate([atoms_ref[to, :CHANNELS, :], atoms_ref[source, :CHANNELS, :]], axis=1)
            atoms = jnp.concatenate([atoms, flags], axis=0)
            pair.append(lax.dot_general(move, atoms, (((1,), (1,)), ((), ())), preferred_element_type=jnp.float32))
        for rank in range(MAXAT):
            tile = jnp.concatenate([moved[rank * LOCAL : (rank + 1) * LOCAL] for moved in pair], axis=0)
            ranked_ref[rank, chip * LOCAL : (chip + 2) * LOCAL, :] = tile.astype(jnp.bfloat16)


def ranked_kernel(own_ref, ranked_ref):
    stays, leaves, _ = share_out(place()[2].astype(jnp.float32), own_ref)
    move_atoms(stays, leaves, own_ref, ranked_ref)


def ranked_call(own):
    vmem = pl.BlockSpec(memory_space=pltpu.VMEM)
    return pl.pallas_call(
        ranked_kernel,
        out_shape=jax.ShapeDtypeStruct((MAXAT, own.shape[0] * LOCAL, CHANNELS + FLAGS), jnp.bfloat16),
        in_specs=[vmem],
        out_specs=vmem,
        compiler_params=pltpu.CompilerParams(vmem_limit_bytes=8 * 1024 * 1024),
        cost_estimate=pl.CostEstimate(flops=40000000, bytes_accessed=1400000, transcendentals=0),
        name="ranked",
    )(own)


def design_kernel(own_ref, other_ref, first_ref, maps_ref, high_ref, low_ref, gram_ref, second_ref, design_ref, crossed_ref):
    core, _, element = place()
    element = element.astype(jnp.float32)
    stays, leaves, held = share_out(element, other_ref)
    ranks = jnp.max(jnp.maximum(held, share_out(element, own_ref)[2])).astype(jnp.int32)
    move_atoms(stays, leaves, other_ref, second_ref)
    over = (((1,), (1,)), ((), ()))
    design_ref[...] = jnp.zeros(design_ref.shape, jnp.float32)
    crossed_ref[...] = jnp.zeros(crossed_ref.shape, jnp.float32)
    pick = lax.broadcasted_iota(jnp.int32, (16, CHANNELS + FLAGS), 1) == CHANNELS
    pick = jnp.where(pick, 1.0, 0.0).astype(jnp.bfloat16)

    def terms(atoms, left):
        columns = maps_ref[left * FACTORS : (left + GROUP) * FACTORS, :]
        values = lax.dot_general(columns, atoms, over, preferred_element_type=jnp.float32)
        product = values[:GROUP]
        for factor in range(1, FACTORS):
            product = product * values[factor * GROUP : (factor + 1) * GROUP]
        return product

    def add_ranks(first, amount):
        atoms = []
        for rank in range(amount):
            own, other = first_ref[first + rank], second_ref[first + rank]
            halves = [jnp.where(core == 0, own, other), jnp.where(core == 0, other, own)]
            operand = jnp.concatenate(halves, axis=0)
            flag = lax.dot_general(pick, operand, over, preferred_element_type=jnp.float32)
            mine = jnp.broadcast_to(flag[:1], (GROUP, STRUCTS)) > 0.5
            atoms.append((operand[:, :CHANNELS], mine))
        for left in range(0, WIDTH, GROUP):
            kept = crossed = None
            for operand, mine in atoms:
                product = terms(operand, left)
                here, there = jnp.where(mine, product, 0.0), jnp.where(mine, 0.0, product)
                kept = here if kept is None else kept + here
                crossed = there if crossed is None else crossed + there
            design_ref[left : left + GROUP, :] += kept
            crossed_ref[left : left + GROUP, :] += crossed

    def add_fours(turn, carry):
        add_ranks(turn * 4, 4)
        return carry

    lax.fori_loop(0, ranks // 4, add_fours, 0)

    @pl.when(ranks % 4 >= 2)
    def _():
        add_ranks(ranks // 4 * 4, 2)

    @pl.when(ranks % 2 == 1)
    def _():
        add_ranks(ranks - 1, 1)

    crossed = [pltpu.roll(crossed_ref[:, at : at + LANES], LANES // 2, 1) for at in range(0, STRUCTS, LANES)]
    design = design_ref[...] + jnp.concatenate(crossed, axis=1)
    high = design.astype(jnp.bfloat16)
    low = (design - high.astype(jnp.float32)).astype(jnp.bfloat16)
    high_ref[...] = high
    low_ref[...] = low
    down = (((0,), (0,)), ((), ()))
    gram = lax.dot_general(high, high, down, preferred_element_type=jnp.float32)
    gram += lax.dot_general(high, low, down, preferred_element_type=jnp.float32)
    gram += lax.dot_general(low, high, down, preferred_element_type=jnp.float32)
    for left in range(0, STRUCTS, LANES):
        gram_ref[left // LANES * STRUCTS : (left // LANES + 1) * STRUCTS, :] = gram[:, left : left + LANES]


def design_call(own, other, ranked, maps):
    vmem = pl.BlockSpec(memory_space=pltpu.VMEM)
    return pl.pallas_call(
        design_kernel,
        out_shape=(
            jax.ShapeDtypeStruct((WIDTH, STRUCTS), jnp.bfloat16),
            jax.ShapeDtypeStruct((WIDTH, STRUCTS), jnp.bfloat16),
            jax.ShapeDtypeStruct((STRUCTS * STRUCTS // LANES, LANES), jnp.float32),
        ),
        in_specs=[vmem] * 4,
        out_specs=(vmem, vmem, vmem),
        scratch_shapes=[
            pltpu.VMEM((MAXAT, STRUCTS // 2, CHANNELS + FLAGS), jnp.bfloat16),
            pltpu.VMEM((WIDTH, STRUCTS), jnp.float32),
            pltpu.VMEM((WIDTH, STRUCTS), jnp.float32),
        ],
        compiler_params=pltpu.CompilerParams(vmem_limit_bytes=24 * 1024 * 1024),
        name="design",
    )(own, other, ranked, maps)


def total_kernel(parts_ref, out_ref):
    parts = parts_ref[...]
    out_ref[...] = jnp.broadcast_to(jnp.sum(parts, axis=0, keepdims=True), parts.shape)


def total_call(parts):
    vmem = pl.BlockSpec(memory_space=pltpu.VMEM)
    return pl.pallas_call(
        total_kernel,
        out_shape=jax.ShapeDtypeStruct(parts.shape, parts.dtype),
        in_specs=[vmem],
        out_specs=vmem,
        compiler_params=pltpu.CompilerParams(vmem_limit_bytes=4 * 1024 * 1024),
        name="total",
    )(parts)


def split(value, amount):
    parts = []
    for _ in range(amount):
        part = value.astype(jnp.bfloat16)
        parts.append(part)
        value = value - part.astype(jnp.float32)
    return parts


def stacked(vector):
    first, second, third = [part.astype(jnp.float32) for part in split(vector, 3)]
    row = lax.broadcasted_iota(jnp.int32, (16, vector.shape[1]), 0)
    one = jnp.where(row == 0, first, 0.0)
    two = jnp.where(row == 1, second, one)
    three = jnp.where(row == 2, third, two)
    return [operand.astype(jnp.bfloat16) for operand in (three, two)]


def picked(own_ref, other_ref, core):
    chips = own_ref.shape[0]
    kinds = (COUNT, ENERGY, ENERGY + 1, ENERGY + 2)
    parts = [half[:, kind, :].astype(jnp.float32) for kind in kinds for half in (own_ref, other_ref)]
    parts = jnp.concatenate(parts, axis=0).astype(jnp.bfloat16)
    structure = lax.broadcasted_iota(jnp.int32, (LANES, STRUCTS), 1)
    repeat = structure % LOCAL == lax.broadcasted_iota(jnp.int32, (LANES, STRUCTS), 0)
    parts = jnp.dot(parts, jnp.where(repeat, 1.0, 0.0).astype(jnp.bfloat16), preferred_element_type=jnp.float32)
    block = lax.broadcasted_iota(jnp.int32, (2 * chips, STRUCTS), 0)
    block = block % chips + jnp.where(block < chips, core, 1 - core) * chips
    here = block == lax.broadcasted_iota(jnp.int32, (2 * chips, STRUCTS), 1) // LOCAL
    rows = [
        jnp.sum(jnp.where(here, parts[kind * 2 * chips : (kind + 1) * 2 * chips], 0.0), axis=0, keepdims=True)
        for kind in range(len(kinds))
    ]
    return rows[0], rows[1] + rows[2] + rows[3]


def solve_kernel(gram_ref, own_ref, other_ref, high_ref, low_ref, coefficients_ref, direction_ref):
    core, number, _ = place()
    counts, energies = picked(own_ref, other_ref, core)
    inverse = 1.0 / counts
    gram = split(jnp.concatenate([gram_ref[:STRUCTS, :], gram_ref[STRUCTS:, :]], axis=1), 2)

    def dot(a, b):
        return jnp.sum(a * b, axis=1, keepdims=True)

    def apply(vector):
        image = jnp.zeros((16, STRUCTS), jnp.float32)
        for operand, part in zip(stacked(vector * inverse), gram):
            image = image + jnp.dot(operand, part, preferred_element_type=jnp.float32)
        return jnp.sum(image, axis=0, keepdims=True) * inverse

    image = apply(energies)
    square = dot(energies, energies)
    shrink = lax.rsqrt(square)
    beta = square * shrink
    left = energies * shrink
    right = left
    image = image * shrink
    square = dot(right, image)
    shrink = lax.rsqrt(square)
    alpha = square * shrink
    right, image = right * shrink, image * shrink
    search, search_image = right, image
    iterate = jnp.zeros_like(right)
    iterate_image = iterate
    phibar = beta
    rhobar = alpha
    for step in range(ITERS):
        left = image - alpha * left
        left_image = apply(left) if step < ITERS - 1 else None
        square = dot(left, left)
        shrink = lax.rsqrt(square)
        beta = square * shrink
        left = left * shrink
        over_rho = lax.rsqrt(rhobar * rhobar + square)
        cosine_part = rhobar * over_rho
        sine_part = beta * over_rho
        advance = cosine_part * phibar * over_rho
        phibar = sine_part * phibar
        iterate = iterate + advance * search
        iterate_image = iterate_image + advance * search_image
        if step < ITERS - 1:
            right = left - beta * right
            image = left_image * shrink - beta * image
            square = dot(right, image)
            shrink = lax.rsqrt(square)
            alpha = square * shrink
            right, image = right * shrink, image * shrink
            turn = sine_part * alpha * over_rho
            rhobar = -cosine_part * alpha
            search = right - turn * search
            search_image = image - turn * search_image
    iterate = iterate * (math.sqrt(K) * lax.rsqrt(dot(iterate, iterate_image))) * inverse
    over = (((1,), (1,)), ((), ()))
    values = jnp.zeros((16, WIDTH), jnp.float32)
    for operand, part in zip(stacked(iterate), (high_ref[...], low_ref[...])):
        values = values + lax.dot_general(operand, part, over, preferred_element_type=jnp.float32)
    values = jnp.sum(values, axis=0, keepdims=True)
    rows = jnp.concatenate([values[:, at : at + LANES] for at in range(0, WIDTH, LANES)], axis=0)
    for copy in range(coefficients_ref.shape[0]):
        coefficients_ref[copy] = rows
    direction = jnp.broadcast_to(left * math.sqrt(STRUCTS), (8, STRUCTS))
    direction_ref[...] = pltpu.roll(direction, lax.rem(STRUCTS - number * LOCAL, STRUCTS), 1)[:1, :LOCAL]


def solve_call(gram, own, other, high, low, copies):
    vmem = pl.BlockSpec(memory_space=pltpu.VMEM)
    return pl.pallas_call(
        solve_kernel,
        out_shape=(
            jax.ShapeDtypeStruct((copies, WIDTH // LANES, LANES), jnp.float32),
            jax.ShapeDtypeStruct((1, LOCAL), jnp.float32),
        ),
        in_specs=[vmem] * 5,
        out_specs=(vmem, vmem),
        compiler_params=pltpu.CompilerParams(vmem_limit_bytes=16 * 1024 * 1024),
        name="solve",
    )(gram, own, other, high, low)


def swap(value):
    return lax.ppermute(value, "core", [(0, 1), (1, 0)])


def body(dist, nbr_species, species, counts, pattern, projections, energies):
    struct = lax.axis_index(STRUCT)
    structs = lax.axis_size(STRUCT)
    owners = projections.shape[2] // WIDTH
    mine = jnp.minimum(struct, owners - 1)

    packed = atomic_call(dist, nbr_species, species, counts, pattern, energies, lax.axis_size("chip"))
    own = lax.all_to_all(packed, "chip", 0, 0)
    maps = maps_call(lax.dynamic_slice_in_dim(projections, mine * WIDTH, WIDTH, 2))
    own, maps = lax.optimization_barrier((own, maps))
    other = swap(own)
    ranked = ranked_call(own)
    high, low, gram = design_call(own, other, ranked, maps)
    everyone = ("chip", "core", "basis")
    parts = lax.all_to_all(gram.reshape(lax.axis_size(everyone), -1, LANES), everyone, 0, 0)
    gram = lax.all_to_all(total_call(parts), everyone, 0, 0).reshape(-1, LANES)
    values, direction = solve_call(gram, own, other, high, low, structs)
    values = lax.all_to_all(values, STRUCT, 0, 0)
    return (values[:owners].reshape(-1), direction.reshape(-1))


def solution(mesh):
    chips = Mesh(mesh.devices.reshape(-1, 2, mesh.shape["basis"]), ("chip", "core", "basis"))
    placed = (
        P(None, STRUCT),
        P(None, STRUCT),
        P(STRUCT),
        P(STRUCT),
        P(),
        P(None, None, "basis"),
        P(STRUCT),
    )
    return jax.shard_map(
        body, mesh=chips, in_specs=placed, out_specs=(P("basis"), P(STRUCT)), check_vma=False
    )
```

```python
import functools
import math

import jax
import jax.numpy as jnp
from jax import lax
from jax.experimental import pallas as pl
from jax.experimental.pallas import tpu as pltpu
from jax.sharding import Mesh, PartitionSpec as P

SPECIES = 8
RADIAL = 8
FACTORS = 4
CHANNELS = 64
K_SPEC = 12544
MAXAT = 16
ITERS = 4
K = 100352
STRUCTS = 256

LANES = 128
WIDTH = 896
PER_SPEC = K_SPEC // WIDTH
LOCAL = 8
BLOCK = LOCAL * MAXAT
PACKED = 72
CODE, COUNT, ENERGY = 64, 65, 66
GROUP = 64
FLAGS = 16

STRUCT = ("chip", "core")
CUTOFF = 5.0
PI_HIGH = 3.140625
PI_MID = 0.0009670257568359375
PI_LOW = math.pi - PI_HIGH - PI_MID
COS_TERMS = tuple((-1.0) ** n / math.factorial(2 * n) for n in range(9))


def cosine(angle):
    turns = jnp.floor(angle * (1.0 / math.pi) + 0.5)
    rest = angle - turns * PI_HIGH
    rest = rest - turns * PI_MID
    rest = rest - turns * PI_LOW
    square = rest * rest
    value = jnp.full_like(square, COS_TERMS[-1])
    for term in COS_TERMS[-2::-1]:
        value = value * square + term
    odd = turns - 2.0 * jnp.floor(turns * 0.5)
    return value * (1.0 - 2.0 * odd)


def atomic_kernel(dist_ref, nbr_ref, species_ref, counts_ref, pattern_ref, energies_ref, out_ref):
    ratio = dist_ref[...] / CUTOFF
    envelope = (1.0 - ratio) * (1.0 - ratio)
    nbr = nbr_ref[...]
    species = species_ref[...]
    radial = []
    for order in range(RADIAL):
        if order == 0:
            radial.append(envelope)
        else:
            radial.append(envelope * cosine((jnp.float32(math.pi) * jnp.float32(order)) * ratio))
    lane = lax.broadcasted_iota(jnp.int32, (SPECIES, LANES), 1)
    row = lax.broadcasted_iota(jnp.int32, (SPECIES, LANES), 0)
    center = jnp.where(species == row, 1.0, 0.0).astype(jnp.bfloat16)
    pattern = pattern_ref[...].astype(jnp.float32).astype(jnp.bfloat16)
    allowed = lax.dot_general(pattern, center, (((0,), (0,)), ((), ())), preferred_element_type=jnp.float32)
    rows = []
    for element in range(SPECIES):
        match = jnp.where(nbr == element, allowed[element : element + 1], 0.0)
        for order in range(RADIAL):
            rows.append(jnp.sum(match * radial[order], axis=0, keepdims=True))
    atomic = jnp.concatenate(rows, axis=0).astype(jnp.bfloat16)

    small = [counts_ref[...].astype(jnp.float32)]
    energy = energies_ref[...]
    for _ in range(3):
        small.append(energy.astype(jnp.bfloat16).astype(jnp.float32))
        energy = energy - small[-1]
    small = jnp.concatenate(small + [jnp.zeros((4, LOCAL), jnp.float32)], axis=0).astype(jnp.bfloat16)
    spots = jnp.concatenate([lane // MAXAT == row, lane == row], axis=1)
    small = jnp.dot(small, jnp.where(spots, 1.0, 0.0).astype(jnp.bfloat16), preferred_element_type=jnp.float32)
    slots = (lane[:1] % MAXAT).astype(jnp.float32)
    code = jnp.where(slots < small[:1, :LANES], species, SPECIES).astype(jnp.float32)
    parts = [code, small[:4, LANES:]]
    parts.append(jnp.zeros((PACKED - CHANNELS - 5, LANES), jnp.float32))
    packed = jnp.concatenate([atomic, jnp.concatenate(parts, axis=0).astype(jnp.bfloat16)], axis=0)
    for copy in range(out_ref.shape[0]):
        out_ref[copy, :, :] = packed


def atomic_call(dist, nbr_species, species, counts, pattern, energies, copies):
    vmem = pl.BlockSpec(memory_space=pltpu.VMEM)
    return pl.pallas_call(
        atomic_kernel,
        out_shape=jax.ShapeDtypeStruct((copies, PACKED, LANES), jnp.bfloat16),
        in_specs=[vmem] * 6,
        out_specs=vmem,
        name="atomic",
    )(dist, nbr_species, species.reshape(1, -1), counts.reshape(1, -1), pattern, energies.reshape(1, -1))


def maps_kernel(maps_ref, out_ref):
    for left in range(0, WIDTH, LANES):
        for factor in range(FACTORS):
            turned = maps_ref[factor, :, left : left + LANES].astype(jnp.float32).T.astype(jnp.bfloat16)
            for half in range(LANES // GROUP):
                row = ((left // GROUP + half) * FACTORS + factor) * GROUP
                out_ref[row : row + GROUP, :] = turned[half * GROUP : (half + 1) * GROUP]


def maps_call(maps):
    vmem = pl.BlockSpec(memory_space=pltpu.VMEM)
    return pl.pallas_call(
        maps_kernel,
        out_shape=jax.ShapeDtypeStruct((FACTORS * WIDTH, CHANNELS), jnp.bfloat16),
        in_specs=[vmem],
        out_specs=vmem,
        compiler_params=pltpu.CompilerParams(vmem_limit_bytes=8 * 1024 * 1024),
        cost_estimate=pl.CostEstimate(flops=0, bytes_accessed=1400000, transcendentals=0),
        name="maps",
    )(maps)


def place():
    core, chips = lax.axis_index("core"), lax.axis_size("chip")
    struct = lax.axis_index("chip") * 2 + core
    owners = SPECIES // lax.axis_size("basis") * PER_SPEC
    element = lax.div(lax.axis_index("basis") * owners + struct, PER_SPEC)
    return core, core * chips + lax.axis_index("chip"), jnp.where(struct < owners, element, SPECIES + 1)


def share_out(element, atoms_ref):
    codes = atoms_ref[:, CODE, :].astype(jnp.float32)
    lane = lax.broadcasted_iota(jnp.int32, codes.shape, 1)
    slot, structure = lane % MAXAT, (lane // MAXAT).astype(jnp.float32)
    chosen = jnp.where(codes == element, 1.0, 0.0)
    upto, since = chosen, chosen
    for reach in (1, 2, 4, 8):
        upto = upto + jnp.where(slot >= reach, pltpu.roll(upto, reach, 1), 0.0)
        since = since + jnp.where(slot < MAXAT - reach, pltpu.roll(since, LANES - reach, 1), 0.0)
    amount = upto + since - chosen
    partner = pltpu.roll(amount, codes.shape[0] // 2, 0)
    held = jnp.floor((amount + partner + 1.0) * 0.5)
    rank = upto - 1.0
    stays = jnp.where((chosen > 0.0) & (rank < held), rank * LOCAL + structure, -1.0)
    leaves = jnp.where((chosen > 0.0) & (rank >= held), (partner + rank - held) * LOCAL + structure, -1.0)
    return stays.astype(jnp.bfloat16), leaves.astype(jnp.bfloat16), held


def move_atoms(stays, leaves, atoms_ref, ranked_ref):
    chips = atoms_ref.shape[0]
    rows = lax.broadcasted_iota(jnp.int32, (BLOCK, LANES), 0).astype(jnp.float32).astype(jnp.bfloat16)
    one, zero = jnp.ones(rows.shape, jnp.bfloat16), jnp.zeros(rows.shape, jnp.bfloat16)
    flags = jnp.concatenate([one[:FLAGS], zero[:FLAGS]], axis=1)

    def hits(target):
        return jnp.where(jnp.broadcast_to(target, rows.shape) == rows, one, zero)

    for chip in range(0, chips, 2):
        pair = []
        for to in (chip, chip + 1):
            source = (to + chips // 2) % chips
            move = jnp.concatenate([hits(stays[to : to + 1, :]), hits(leaves[source : source + 1, :])], axis=1)
            atoms = jnp.concatenate([atoms_ref[to, :CHANNELS, :], atoms_ref[source, :CHANNELS, :]], axis=1)
            atoms = jnp.concatenate([atoms, flags], axis=0)
            pair.append(lax.dot_general(move, atoms, (((1,), (1,)), ((), ())), preferred_element_type=jnp.float32))
        for rank in range(MAXAT):
            tile = jnp.concatenate([moved[rank * LOCAL : (rank + 1) * LOCAL] for moved in pair], axis=0)
            ranked_ref[rank, chip * LOCAL : (chip + 2) * LOCAL, :] = tile.astype(jnp.bfloat16)


def ranked_kernel(own_ref, ranked_ref):
    stays, leaves, _ = share_out(place()[2].astype(jnp.float32), own_ref)
    move_atoms(stays, leaves, own_ref, ranked_ref)


def ranked_call(own):
    vmem = pl.BlockSpec(memory_space=pltpu.VMEM)
    return pl.pallas_call(
        ranked_kernel,
        out_shape=jax.ShapeDtypeStruct((MAXAT, own.shape[0] * LOCAL, CHANNELS + FLAGS), jnp.bfloat16),
        in_specs=[vmem],
        out_specs=vmem,
        compiler_params=pltpu.CompilerParams(vmem_limit_bytes=8 * 1024 * 1024),
        cost_estimate=pl.CostEstimate(flops=40000000, bytes_accessed=1400000, transcendentals=0),
        name="ranked",
    )(own)


def design_kernel(own_ref, other_ref, first_ref, maps_ref, high_ref, low_ref, gram_ref, second_ref, design_ref, crossed_ref):
    core, _, element = place()
    element = element.astype(jnp.float32)
    stays, leaves, held = share_out(element, other_ref)
    ranks = jnp.max(jnp.maximum(held, share_out(element, own_ref)[2])).astype(jnp.int32)
    move_atoms(stays, leaves, other_ref, second_ref)
    over = (((1,), (1,)), ((), ()))
    pick = lax.broadcasted_iota(jnp.int32, (16, CHANNELS + FLAGS), 1) == CHANNELS
    pick = jnp.where(pick, 1.0, 0.0).astype(jnp.bfloat16)

    def terms(atoms, left):
        columns = maps_ref[left * FACTORS : (left + GROUP) * FACTORS, :]
        values = lax.dot_general(columns, atoms, over, preferred_element_type=jnp.float32)
        product = values[:GROUP]
        for factor in range(1, FACTORS):
            product = product * values[factor * GROUP : (factor + 1) * GROUP]
        return product

    def add_ranks(first, amount, fresh):
        atoms = []
        for rank in range(amount):
            own, other = first_ref[first + rank], second_ref[first + rank]
            halves = [jnp.where(core == 0, own, other), jnp.where(core == 0, other, own)]
            operand = jnp.concatenate(halves, axis=0)
            flag = lax.dot_general(pick, operand, over, preferred_element_type=jnp.float32)
            mine = jnp.broadcast_to(flag[:1], (GROUP, STRUCTS)) > 0.5
            atoms.append((operand[:, :CHANNELS], mine))
        for left in range(0, WIDTH, GROUP):
            kept = crossed = None
            for operand, mine in atoms:
                product = terms(operand, left)
                here, there = jnp.where(mine, product, 0.0), jnp.where(mine, 0.0, product)
                kept = here if kept is None else kept + here
                crossed = there if crossed is None else crossed + there
            rows = slice(left, left + GROUP)
            design_ref[rows, :] = kept if fresh else design_ref[rows, :] + kept
            crossed_ref[rows, :] = crossed if fresh else crossed_ref[rows, :] + crossed

    odd = ranks % 4

    @pl.when(odd == 0)
    def _():
        design_ref[...] = jnp.zeros(design_ref.shape, jnp.float32)
        crossed_ref[...] = jnp.zeros(crossed_ref.shape, jnp.float32)

    for amount in range(1, 4):

        @pl.when(odd == amount)
        def _():
            add_ranks(0, amount, True)

    def add_fours(turn, carry):
        add_ranks(odd + turn * 4, 4, False)
        return carry

    lax.fori_loop(0, ranks // 4, add_fours, 0)
    crossed = [pltpu.roll(crossed_ref[:, at : at + LANES], LANES // 2, 1) for at in range(0, STRUCTS, LANES)]
    design = design_ref[...] + jnp.concatenate(crossed, axis=1)
    high = design.astype(jnp.bfloat16)
    low = (design - high.astype(jnp.float32)).astype(jnp.bfloat16)
    high_ref[...] = high
    low_ref[...] = low
    down = (((0,), (0,)), ((), ()))
    gram = lax.dot_general(high, high, down, preferred_element_type=jnp.float32)
    gram += lax.dot_general(high, low, down, preferred_element_type=jnp.float32)
    gram += lax.dot_general(low, high, down, preferred_element_type=jnp.float32)
    for left in range(0, STRUCTS, LANES):
        gram_ref[left // LANES * STRUCTS : (left // LANES + 1) * STRUCTS, :] = gram[:, left : left + LANES]


def design_call(own, other, ranked, maps):
    vmem = pl.BlockSpec(memory_space=pltpu.VMEM)
    return pl.pallas_call(
        design_kernel,
        out_shape=(
            jax.ShapeDtypeStruct((WIDTH, STRUCTS), jnp.bfloat16),
            jax.ShapeDtypeStruct((WIDTH, STRUCTS), jnp.bfloat16),
            jax.ShapeDtypeStruct((STRUCTS * STRUCTS // LANES, LANES), jnp.float32),
        ),
        in_specs=[vmem] * 4,
        out_specs=(vmem, vmem, vmem),
        scratch_shapes=[
            pltpu.VMEM((MAXAT, STRUCTS // 2, CHANNELS + FLAGS), jnp.bfloat16),
            pltpu.VMEM((WIDTH, STRUCTS), jnp.float32),
            pltpu.VMEM((WIDTH, STRUCTS), jnp.float32),
        ],
        compiler_params=pltpu.CompilerParams(vmem_limit_bytes=24 * 1024 * 1024),
        name="design",
    )(own, other, ranked, maps)


def total_kernel(parts_ref, out_ref):
    parts = parts_ref[...]
    out_ref[...] = jnp.broadcast_to(jnp.sum(parts, axis=0, keepdims=True), parts.shape)


def total_call(parts):
    vmem = pl.BlockSpec(memory_space=pltpu.VMEM)
    return pl.pallas_call(
        total_kernel,
        out_shape=jax.ShapeDtypeStruct(parts.shape, parts.dtype),
        in_specs=[vmem],
        out_specs=vmem,
        compiler_params=pltpu.CompilerParams(vmem_limit_bytes=4 * 1024 * 1024),
        name="total",
    )(parts)


def split(value, amount):
    parts = []
    for _ in range(amount):
        part = value.astype(jnp.bfloat16)
        parts.append(part)
        value = value - part.astype(jnp.float32)
    return parts


def stacked(vector):
    first, second, third = [part.astype(jnp.float32) for part in split(vector, 3)]
    row = lax.broadcasted_iota(jnp.int32, (16, vector.shape[1]), 0)
    one = jnp.where(row == 0, first, 0.0)
    two = jnp.where(row == 1, second, one)
    three = jnp.where(row == 2, third, two)
    return [operand.astype(jnp.bfloat16) for operand in (three, two)]


def picked(own_ref, other_ref, core):
    chips = own_ref.shape[0]
    kinds = (COUNT, ENERGY, ENERGY + 1, ENERGY + 2)
    parts = [half[:, kind, :].astype(jnp.float32) for kind in kinds for half in (own_ref, other_ref)]
    parts = jnp.concatenate(parts, axis=0).astype(jnp.bfloat16)
    structure = lax.broadcasted_iota(jnp.int32, (LANES, STRUCTS), 1)
    repeat = structure % LOCAL == lax.broadcasted_iota(jnp.int32, (LANES, STRUCTS), 0)
    parts = jnp.dot(parts, jnp.where(repeat, 1.0, 0.0).astype(jnp.bfloat16), preferred_element_type=jnp.float32)
    block = lax.broadcasted_iota(jnp.int32, (2 * chips, STRUCTS), 0)
    block = block % chips + jnp.where(block < chips, core, 1 - core) * chips
    here = block == lax.broadcasted_iota(jnp.int32, (2 * chips, STRUCTS), 1) // LOCAL
    rows = [
        jnp.sum(jnp.where(here, parts[kind * 2 * chips : (kind + 1) * 2 * chips], 0.0), axis=0, keepdims=True)
        for kind in range(len(kinds))
    ]
    return rows[0], rows[1] + rows[2] + rows[3]


def solve_kernel(gram_ref, own_ref, other_ref, high_ref, low_ref, coefficients_ref, direction_ref):
    core, number, _ = place()
    counts, energies = picked(own_ref, other_ref, core)
    inverse = 1.0 / counts
    gram = split(jnp.concatenate([gram_ref[:STRUCTS, :], gram_ref[STRUCTS:, :]], axis=1), 2)

    def dot(a, b):
        return jnp.sum(a * b, axis=1, keepdims=True)

    def apply(vector):
        image = jnp.zeros((16, STRUCTS), jnp.float32)
        for operand, part in zip(stacked(vector * inverse), gram):
            image = image + jnp.dot(operand, part, preferred_element_type=jnp.float32)
        return jnp.sum(image, axis=0, keepdims=True) * inverse

    image = apply(energies)
    square = dot(energies, energies)
    shrink = lax.rsqrt(square)
    beta = square * shrink
    left = energies * shrink
    right = left
    image = image * shrink
    square = dot(right, image)
    shrink = lax.rsqrt(square)
    alpha = square * shrink
    right, image = right * shrink, image * shrink
    search, search_image = right, image
    iterate = jnp.zeros_like(right)
    iterate_image = iterate
    phibar = beta
    rhobar = alpha
    for step in range(ITERS):
        left = image - alpha * left
        left_image = apply(left) if step < ITERS - 1 else None
        square = dot(left, left)
        shrink = lax.rsqrt(square)
        beta = square * shrink
        left = left * shrink
        over_rho = lax.rsqrt(rhobar * rhobar + square)
        cosine_part = rhobar * over_rho
        sine_part = beta * over_rho
        advance = cosine_part * phibar * over_rho
        phibar = sine_part * phibar
        iterate = iterate + advance * search
        iterate_image = iterate_image + advance * search_image
        if step < ITERS - 1:
            right = left - beta * right
            image = left_image * shrink - beta * image
            square = dot(right, image)
            shrink = lax.rsqrt(square)
            alpha = square * shrink
            right, image = right * shrink, image * shrink
            turn = sine_part * alpha * over_rho
            rhobar = -cosine_part * alpha
            search = right - turn * search
            search_image = image - turn * search_image
    iterate = iterate * (math.sqrt(K) * lax.rsqrt(dot(iterate, iterate_image))) * inverse
    over = (((1,), (1,)), ((), ()))
    values = jnp.zeros((16, WIDTH), jnp.float32)
    for operand, part in zip(stacked(iterate), (high_ref[...], low_ref[...])):
        values = values + lax.dot_general(operand, part, over, preferred_element_type=jnp.float32)
    values = jnp.sum(values, axis=0, keepdims=True)
    rows = jnp.concatenate([values[:, at : at + LANES] for at in range(0, WIDTH, LANES)], axis=0)
    for copy in range(coefficients_ref.shape[0]):
        coefficients_ref[copy] = rows
    direction = jnp.broadcast_to(left * math.sqrt(STRUCTS), (8, STRUCTS))
    direction_ref[...] = pltpu.roll(direction, lax.rem(STRUCTS - number * LOCAL, STRUCTS), 1)[:1, :LOCAL]


def solve_call(gram, own, other, high, low, copies):
    vmem = pl.BlockSpec(memory_space=pltpu.VMEM)
    return pl.pallas_call(
        solve_kernel,
        out_shape=(
            jax.ShapeDtypeStruct((copies, WIDTH // LANES, LANES), jnp.float32),
            jax.ShapeDtypeStruct((1, LOCAL), jnp.float32),
        ),
        in_specs=[vmem] * 5,
        out_specs=(vmem, vmem),
        compiler_params=pltpu.CompilerParams(vmem_limit_bytes=16 * 1024 * 1024),
        name="solve",
    )(gram, own, other, high, low)


def swap(value):
    return lax.ppermute(value, "core", [(0, 1), (1, 0)])


def body(dist, nbr_species, species, counts, pattern, projections, energies):
    struct = lax.axis_index(STRUCT)
    structs = lax.axis_size(STRUCT)
    owners = projections.shape[2] // WIDTH
    mine = jnp.minimum(struct, owners - 1)

    packed = atomic_call(dist, nbr_species, species, counts, pattern, energies, lax.axis_size("chip"))
    own = lax.all_to_all(packed, "chip", 0, 0)
    maps = maps_call(lax.dynamic_slice_in_dim(projections, mine * WIDTH, WIDTH, 2))
    own, maps = lax.optimization_barrier((own, maps))
    other = swap(own)
    ranked = ranked_call(own)
    high, low, gram = design_call(own, other, ranked, maps)
    everyone = ("basis", "chip", "core")
    parts = lax.all_to_all(gram.reshape(lax.axis_size(everyone), -1, LANES), everyone, 0, 0)
    gram = lax.all_to_all(total_call(parts), everyone, 0, 0).reshape(-1, LANES)
    values, direction = solve_call(gram, own, other, high, low, structs)
    values = lax.all_to_all(values, STRUCT, 0, 0)
    return (values[:owners].reshape(-1), direction.reshape(-1))


def solution(mesh):
    chips = Mesh(mesh.devices.reshape(-1, 2, mesh.shape["basis"]), ("chip", "core", "basis"))
    placed = (
        P(None, STRUCT),
        P(None, STRUCT),
        P(STRUCT),
        P(STRUCT),
        P(),
        P(None, None, "basis"),
        P(STRUCT),
    )
    return jax.shard_map(
        body, mesh=chips, in_specs=placed, out_specs=(P("basis"), P(STRUCT)), check_vma=False
    )
```

```python
import functools
import math

import jax
import jax.numpy as jnp
from jax import lax
from jax.experimental import pallas as pl
from jax.experimental.pallas import tpu as pltpu
from jax.sharding import Mesh, PartitionSpec as P

SPECIES = 8
RADIAL = 8
FACTORS = 4
CHANNELS = 64
K_SPEC = 12544
MAXAT = 16
ITERS = 4
K = 100352
STRUCTS = 256

LANES = 128
WIDTH = 896
PER_SPEC = K_SPEC // WIDTH
LOCAL = 8
BLOCK = LOCAL * MAXAT
PACKED = 72
CODE, COUNT, ENERGY = 64, 65, 66
GROUP = 64
FLAGS = 16

STRUCT = ("chip", "core")
CUTOFF = 5.0
PI_HIGH = 3.140625
PI_MID = 0.0009670257568359375
PI_LOW = math.pi - PI_HIGH - PI_MID
COS_TERMS = tuple((-1.0) ** n / math.factorial(2 * n) for n in range(9))


def cosine(angle):
    turns = jnp.floor(angle * (1.0 / math.pi) + 0.5)
    rest = angle - turns * PI_HIGH
    rest = rest - turns * PI_MID
    rest = rest - turns * PI_LOW
    square = rest * rest
    value = jnp.full_like(square, COS_TERMS[-1])
    for term in COS_TERMS[-2::-1]:
        value = value * square + term
    odd = turns - 2.0 * jnp.floor(turns * 0.5)
    return value * (1.0 - 2.0 * odd)


def atomic_kernel(dist_ref, nbr_ref, species_ref, counts_ref, pattern_ref, energies_ref, out_ref):
    ratio = dist_ref[...] / CUTOFF
    envelope = (1.0 - ratio) * (1.0 - ratio)
    nbr = nbr_ref[...]
    species = species_ref[...]
    radial = []
    for order in range(RADIAL):
        if order == 0:
            radial.append(envelope)
        else:
            radial.append(envelope * cosine((jnp.float32(math.pi) * jnp.float32(order)) * ratio))
    lane = lax.broadcasted_iota(jnp.int32, (SPECIES, LANES), 1)
    row = lax.broadcasted_iota(jnp.int32, (SPECIES, LANES), 0)
    center = jnp.where(species == row, 1.0, 0.0).astype(jnp.bfloat16)
    pattern = pattern_ref[...].astype(jnp.float32).astype(jnp.bfloat16)
    allowed = lax.dot_general(pattern, center, (((0,), (0,)), ((), ())), preferred_element_type=jnp.float32)
    rows = []
    for element in range(SPECIES):
        match = jnp.where(nbr == element, allowed[element : element + 1], 0.0)
        for order in range(RADIAL):
            rows.append(jnp.sum(match * radial[order], axis=0, keepdims=True))
    atomic = jnp.concatenate(rows, axis=0).astype(jnp.bfloat16)

    small = [counts_ref[...].astype(jnp.float32)]
    energy = energies_ref[...]
    for _ in range(3):
        small.append(energy.astype(jnp.bfloat16).astype(jnp.float32))
        energy = energy - small[-1]
    small = jnp.concatenate(small + [jnp.zeros((4, LOCAL), jnp.float32)], axis=0).astype(jnp.bfloat16)
    spots = jnp.concatenate([lane // MAXAT == row, lane == row], axis=1)
    small = jnp.dot(small, jnp.where(spots, 1.0, 0.0).astype(jnp.bfloat16), preferred_element_type=jnp.float32)
    slots = (lane[:1] % MAXAT).astype(jnp.float32)
    code = jnp.where(slots < small[:1, :LANES], species, SPECIES).astype(jnp.float32)
    parts = [code, small[:4, LANES:]]
    parts.append(jnp.zeros((PACKED - CHANNELS - 5, LANES), jnp.float32))
    packed = jnp.concatenate([atomic, jnp.concatenate(parts, axis=0).astype(jnp.bfloat16)], axis=0)
    for copy in range(out_ref.shape[0]):
        out_ref[copy, :, :] = packed


def atomic_call(dist, nbr_species, species, counts, pattern, energies, copies):
    vmem = pl.BlockSpec(memory_space=pltpu.VMEM)
    return pl.pallas_call(
        atomic_kernel,
        out_shape=jax.ShapeDtypeStruct((copies, PACKED, LANES), jnp.bfloat16),
        in_specs=[vmem] * 6,
        out_specs=vmem,
        name="atomic",
    )(dist, nbr_species, species.reshape(1, -1), counts.reshape(1, -1), pattern, energies.reshape(1, -1))


def maps_kernel(maps_ref, out_ref):
    for left in range(0, WIDTH, LANES):
        for factor in range(FACTORS):
            turned = maps_ref[factor, :, left : left + LANES].astype(jnp.float32).T.astype(jnp.bfloat16)
            for half in range(LANES // GROUP):
                row = ((left // GROUP + half) * FACTORS + factor) * GROUP
                out_ref[row : row + GROUP, :] = turned[half * GROUP : (half + 1) * GROUP]


def maps_call(maps):
    vmem = pl.BlockSpec(memory_space=pltpu.VMEM)
    return pl.pallas_call(
        maps_kernel,
        out_shape=jax.ShapeDtypeStruct((FACTORS * WIDTH, CHANNELS), jnp.bfloat16),
        in_specs=[vmem],
        out_specs=vmem,
        compiler_params=pltpu.CompilerParams(vmem_limit_bytes=8 * 1024 * 1024),
        cost_estimate=pl.CostEstimate(flops=0, bytes_accessed=1400000, transcendentals=0),
        name="maps",
    )(maps)


def place():
    core, chips = lax.axis_index("core"), lax.axis_size("chip")
    struct = lax.axis_index("chip") * 2 + core
    owners = SPECIES // lax.axis_size("basis") * PER_SPEC
    element = lax.div(lax.axis_index("basis") * owners + struct, PER_SPEC)
    return core, core * chips + lax.axis_index("chip"), jnp.where(struct < owners, element, SPECIES + 1)


def share_out(element, atoms_ref):
    codes = atoms_ref[:, CODE, :].astype(jnp.float32)
    lane = lax.broadcasted_iota(jnp.int32, codes.shape, 1)
    slot, structure = lane % MAXAT, (lane // MAXAT).astype(jnp.float32)
    chosen = jnp.where(codes == element, 1.0, 0.0)
    upto, since = chosen, chosen
    for reach in (1, 2, 4, 8):
        upto = upto + jnp.where(slot >= reach, pltpu.roll(upto, reach, 1), 0.0)
        since = since + jnp.where(slot < MAXAT - reach, pltpu.roll(since, LANES - reach, 1), 0.0)
    amount = upto + since - chosen
    partner = pltpu.roll(amount, codes.shape[0] // 2, 0)
    held = jnp.floor((amount + partner + 1.0) * 0.5)
    rank = upto - 1.0
    stays = jnp.where((chosen > 0.0) & (rank < held), rank * LOCAL + structure, -1.0)
    leaves = jnp.where((chosen > 0.0) & (rank >= held), (partner + rank - held) * LOCAL + structure, -1.0)
    return stays.astype(jnp.bfloat16), leaves.astype(jnp.bfloat16), held


def move_atoms(stays, leaves, atoms_ref, ranked_ref):
    chips = atoms_ref.shape[0]
    rows = lax.broadcasted_iota(jnp.int32, (BLOCK, LANES), 0).astype(jnp.float32).astype(jnp.bfloat16)
    one, zero = jnp.ones(rows.shape, jnp.bfloat16), jnp.zeros(rows.shape, jnp.bfloat16)
    flags = jnp.concatenate([one[:FLAGS], zero[:FLAGS]], axis=1)

    def hits(target):
        return jnp.where(jnp.broadcast_to(target, rows.shape) == rows, one, zero)

    for chip in range(0, chips, 2):
        pair = []
        for to in (chip, chip + 1):
            source = (to + chips // 2) % chips
            move = jnp.concatenate([hits(stays[to : to + 1, :]), hits(leaves[source : source + 1, :])], axis=1)
            atoms = jnp.concatenate([atoms_ref[to, :CHANNELS, :], atoms_ref[source, :CHANNELS, :]], axis=1)
            atoms = jnp.concatenate([atoms, flags], axis=0)
            pair.append(lax.dot_general(move, atoms, (((1,), (1,)), ((), ())), preferred_element_type=jnp.float32))
        for rank in range(MAXAT):
            tile = jnp.concatenate([moved[rank * LOCAL : (rank + 1) * LOCAL] for moved in pair], axis=0)
            ranked_ref[rank, chip * LOCAL : (chip + 2) * LOCAL, :] = tile.astype(jnp.bfloat16)


def ranked_kernel(own_ref, ranked_ref, held_ref):
    stays, leaves, held_ref[...] = share_out(place()[2].astype(jnp.float32), own_ref)
    move_atoms(stays, leaves, own_ref, ranked_ref)


def ranked_call(own):
    vmem = pl.BlockSpec(memory_space=pltpu.VMEM)
    return pl.pallas_call(
        ranked_kernel,
        out_shape=(
            jax.ShapeDtypeStruct((MAXAT, own.shape[0] * LOCAL, CHANNELS + FLAGS), jnp.bfloat16),
            jax.ShapeDtypeStruct((own.shape[0], LANES), jnp.float32),
        ),
        in_specs=[vmem],
        out_specs=(vmem, vmem),
        compiler_params=pltpu.CompilerParams(vmem_limit_bytes=8 * 1024 * 1024),
        cost_estimate=pl.CostEstimate(flops=40000000, bytes_accessed=1400000, transcendentals=0),
        name="ranked",
    )(own)


def design_kernel(held_ref, other_ref, first_ref, maps_ref, high_ref, low_ref, gram_ref, second_ref, design_ref, crossed_ref):
    core, _, element = place()
    element = element.astype(jnp.float32)
    stays, leaves, held = share_out(element, other_ref)
    ranks = jnp.max(jnp.maximum(held, held_ref[...])).astype(jnp.int32)
    move_atoms(stays, leaves, other_ref, second_ref)
    over = (((1,), (1,)), ((), ()))
    pick = lax.broadcasted_iota(jnp.int32, (16, CHANNELS + FLAGS), 1) == CHANNELS
    pick = jnp.where(pick, 1.0, 0.0).astype(jnp.bfloat16)

    def terms(atoms, left):
        columns = maps_ref[left * FACTORS : (left + GROUP) * FACTORS, :]
        values = lax.dot_general(columns, atoms, over, preferred_element_type=jnp.float32)
        product = values[:GROUP]
        for factor in range(1, FACTORS):
            product = product * values[factor * GROUP : (factor + 1) * GROUP]
        return product

    def add_ranks(first, amount, fresh):
        atoms = []
        for rank in range(amount):
            own, other = first_ref[first + rank], second_ref[first + rank]
            halves = [jnp.where(core == 0, own, other), jnp.where(core == 0, other, own)]
            operand = jnp.concatenate(halves, axis=0)
            flag = lax.dot_general(pick, operand, over, preferred_element_type=jnp.float32)
            mine = jnp.broadcast_to(flag[:1], (GROUP, STRUCTS)) > 0.5
            atoms.append((operand[:, :CHANNELS], mine))
        for left in range(0, WIDTH, GROUP):
            kept = crossed = None
            for operand, mine in atoms:
                product = terms(operand, left)
                here, there = jnp.where(mine, product, 0.0), jnp.where(mine, 0.0, product)
                kept = here if kept is None else kept + here
                crossed = there if crossed is None else crossed + there
            rows = slice(left, left + GROUP)
            design_ref[rows, :] = kept if fresh else design_ref[rows, :] + kept
            crossed_ref[rows, :] = crossed if fresh else crossed_ref[rows, :] + crossed

    odd = ranks % 4

    @pl.when(odd == 0)
    def _():
        design_ref[...] = jnp.zeros(design_ref.shape, jnp.float32)
        crossed_ref[...] = jnp.zeros(crossed_ref.shape, jnp.float32)

    for amount in range(1, 4):

        @pl.when(odd == amount)
        def _():
            add_ranks(0, amount, True)

    def add_fours(turn, carry):
        add_ranks(odd + turn * 4, 4, False)
        return carry

    lax.fori_loop(0, ranks // 4, add_fours, 0)
    crossed = [pltpu.roll(crossed_ref[:, at : at + LANES], LANES // 2, 1) for at in range(0, STRUCTS, LANES)]
    design = design_ref[...] + jnp.concatenate(crossed, axis=1)
    high = design.astype(jnp.bfloat16)
    low = (design - high.astype(jnp.float32)).astype(jnp.bfloat16)
    high_ref[...] = high
    low_ref[...] = low
    down = (((0,), (0,)), ((), ()))
    gram = lax.dot_general(high, high, down, preferred_element_type=jnp.float32)
    gram += lax.dot_general(high, low, down, preferred_element_type=jnp.float32)
    gram += lax.dot_general(low, high, down, preferred_element_type=jnp.float32)
    for left in range(0, STRUCTS, LANES):
        gram_ref[left // LANES * STRUCTS : (left // LANES + 1) * STRUCTS, :] = gram[:, left : left + LANES]


def design_call(held, other, ranked, maps):
    vmem = pl.BlockSpec(memory_space=pltpu.VMEM)
    return pl.pallas_call(
        design_kernel,
        out_shape=(
            jax.ShapeDtypeStruct((WIDTH, STRUCTS), jnp.bfloat16),
            jax.ShapeDtypeStruct((WIDTH, STRUCTS), jnp.bfloat16),
            jax.ShapeDtypeStruct((STRUCTS * STRUCTS // LANES, LANES), jnp.float32),
        ),
        in_specs=[vmem] * 4,
        out_specs=(vmem, vmem, vmem),
        scratch_shapes=[
            pltpu.VMEM((MAXAT, STRUCTS // 2, CHANNELS + FLAGS), jnp.bfloat16),
            pltpu.VMEM((WIDTH, STRUCTS), jnp.float32),
            pltpu.VMEM((WIDTH, STRUCTS), jnp.float32),
        ],
        compiler_params=pltpu.CompilerParams(vmem_limit_bytes=24 * 1024 * 1024),
        name="design",
    )(held, other, ranked, maps)


def total_kernel(parts_ref, out_ref):
    parts = parts_ref[...]
    out_ref[...] = jnp.broadcast_to(jnp.sum(parts, axis=0, keepdims=True), parts.shape)


def total_call(parts):
    vmem = pl.BlockSpec(memory_space=pltpu.VMEM)
    return pl.pallas_call(
        total_kernel,
        out_shape=jax.ShapeDtypeStruct(parts.shape, parts.dtype),
        in_specs=[vmem],
        out_specs=vmem,
        compiler_params=pltpu.CompilerParams(vmem_limit_bytes=4 * 1024 * 1024),
        name="total",
    )(parts)


def split(value, amount):
    parts = []
    for _ in range(amount):
        part = value.astype(jnp.bfloat16)
        parts.append(part)
        value = value - part.astype(jnp.float32)
    return parts


def stacked(vector):
    first, second, third = [part.astype(jnp.float32) for part in split(vector, 3)]
    row = lax.broadcasted_iota(jnp.int32, (16, vector.shape[1]), 0)
    one = jnp.where(row == 0, first, 0.0)
    two = jnp.where(row == 1, second, one)
    three = jnp.where(row == 2, third, two)
    return [operand.astype(jnp.bfloat16) for operand in (three, two)]


def picked(own_ref, other_ref, core):
    chips = own_ref.shape[0]
    kinds = (COUNT, ENERGY, ENERGY + 1, ENERGY + 2)
    parts = [half[:, kind, :].astype(jnp.float32) for kind in kinds for half in (own_ref, other_ref)]
    parts = jnp.concatenate(parts, axis=0).astype(jnp.bfloat16)
    structure = lax.broadcasted_iota(jnp.int32, (LANES, STRUCTS), 1)
    repeat = structure % LOCAL == lax.broadcasted_iota(jnp.int32, (LANES, STRUCTS), 0)
    parts = jnp.dot(parts, jnp.where(repeat, 1.0, 0.0).astype(jnp.bfloat16), preferred_element_type=jnp.float32)
    block = lax.broadcasted_iota(jnp.int32, (2 * chips, STRUCTS), 0)
    block = block % chips + jnp.where(block < chips, core, 1 - core) * chips
    here = block == lax.broadcasted_iota(jnp.int32, (2 * chips, STRUCTS), 1) // LOCAL
    rows = [
        jnp.sum(jnp.where(here, parts[kind * 2 * chips : (kind + 1) * 2 * chips], 0.0), axis=0, keepdims=True)
        for kind in range(len(kinds))
    ]
    return rows[0], rows[1] + rows[2] + rows[3]


def solve_kernel(gram_ref, own_ref, other_ref, high_ref, low_ref, coefficients_ref, direction_ref):
    core, number, _ = place()
    counts, energies = picked(own_ref, other_ref, core)
    inverse = 1.0 / counts
    gram = split(jnp.concatenate([gram_ref[:STRUCTS, :], gram_ref[STRUCTS:, :]], axis=1), 2)

    def dot(a, b):
        return jnp.sum(a * b, axis=1, keepdims=True)

    def apply(vector):
        image = jnp.zeros((16, STRUCTS), jnp.float32)
        for operand, part in zip(stacked(vector * inverse), gram):
            image = image + jnp.dot(operand, part, preferred_element_type=jnp.float32)
        return jnp.sum(image, axis=0, keepdims=True) * inverse

    image = apply(energies)
    square = dot(energies, energies)
    shrink = lax.rsqrt(square)
    beta = square * shrink
    left = energies * shrink
    right = left
    image = image * shrink
    square = dot(right, image)
    shrink = lax.rsqrt(square)
    alpha = square * shrink
    right, image = right * shrink, image * shrink
    search, search_image = right, image
    iterate = jnp.zeros_like(right)
    iterate_image = iterate
    phibar = beta
    rhobar = alpha
    for step in range(ITERS):
        left = image - alpha * left
        left_image = apply(left) if step < ITERS - 1 else None
        square = dot(left, left)
        shrink = lax.rsqrt(square)
        beta = square * shrink
        left = left * shrink
        over_rho = lax.rsqrt(rhobar * rhobar + square)
        cosine_part = rhobar * over_rho
        sine_part = beta * over_rho
        advance = cosine_part * phibar * over_rho
        phibar = sine_part * phibar
        iterate = iterate + advance * search
        iterate_image = iterate_image + advance * search_image
        if step < ITERS - 1:
            right = left - beta * right
            image = left_image * shrink - beta * image
            square = dot(right, image)
            shrink = lax.rsqrt(square)
            alpha = square * shrink
            right, image = right * shrink, image * shrink
            turn = sine_part * alpha * over_rho
            rhobar = -cosine_part * alpha
            search = right - turn * search
            search_image = image - turn * search_image
    iterate = iterate * (math.sqrt(K) * lax.rsqrt(dot(iterate, iterate_image))) * inverse
    over = (((1,), (1,)), ((), ()))
    values = jnp.zeros((16, WIDTH), jnp.float32)
    for operand, part in zip(stacked(iterate), (high_ref[...], low_ref[...])):
        values = values + lax.dot_general(operand, part, over, preferred_element_type=jnp.float32)
    values = jnp.sum(values, axis=0, keepdims=True)
    rows = jnp.concatenate([values[:, at : at + LANES] for at in range(0, WIDTH, LANES)], axis=0)
    for copy in range(coefficients_ref.shape[0]):
        coefficients_ref[copy] = rows
    direction = jnp.broadcast_to(left * math.sqrt(STRUCTS), (8, STRUCTS))
    direction_ref[...] = pltpu.roll(direction, lax.rem(STRUCTS - number * LOCAL, STRUCTS), 1)[:1, :LOCAL]


def solve_call(gram, own, other, high, low, copies):
    vmem = pl.BlockSpec(memory_space=pltpu.VMEM)
    return pl.pallas_call(
        solve_kernel,
        out_shape=(
            jax.ShapeDtypeStruct((copies, WIDTH // LANES, LANES), jnp.float32),
            jax.ShapeDtypeStruct((1, LOCAL), jnp.float32),
        ),
        in_specs=[vmem] * 5,
        out_specs=(vmem, vmem),
        compiler_params=pltpu.CompilerParams(vmem_limit_bytes=16 * 1024 * 1024),
        name="solve",
    )(gram, own, other, high, low)


def swap(value):
    return lax.ppermute(value, "core", [(0, 1), (1, 0)])


def body(dist, nbr_species, species, counts, pattern, projections, energies):
    struct = lax.axis_index(STRUCT)
    structs = lax.axis_size(STRUCT)
    owners = projections.shape[2] // WIDTH
    mine = jnp.minimum(struct, owners - 1)

    packed = atomic_call(dist, nbr_species, species, counts, pattern, energies, lax.axis_size("chip"))
    own = lax.all_to_all(packed, "chip", 0, 0)
    maps = maps_call(lax.dynamic_slice_in_dim(projections, mine * WIDTH, WIDTH, 2))
    own, maps = lax.optimization_barrier((own, maps))
    other = swap(own)
    ranked, held = ranked_call(own)
    high, low, gram = design_call(held, other, ranked, maps)
    everyone = ("chip", "core", "basis")
    parts = lax.all_to_all(gram.reshape(lax.axis_size(everyone), -1, LANES), everyone, 0, 0)
    gram = lax.all_to_all(total_call(parts), everyone, 0, 0).reshape(-1, LANES)
    values, direction = solve_call(gram, own, other, high, low, structs)
    values = lax.all_to_all(values, STRUCT, 0, 0)
    return (values[:owners].reshape(-1), direction.reshape(-1))


def solution(mesh):
    chips = Mesh(mesh.devices.reshape(-1, 2, mesh.shape["basis"]), ("chip", "core", "basis"))
    placed = (
        P(None, STRUCT),
        P(None, STRUCT),
        P(STRUCT),
        P(STRUCT),
        P(),
        P(None, None, "basis"),
        P(STRUCT),
    )
    return jax.shard_map(
        body, mesh=chips, in_specs=placed, out_specs=(P("basis"), P(STRUCT)), check_vma=False
    )
```

```python
import functools
import math

import jax
import jax.numpy as jnp
from jax import lax
from jax.experimental import pallas as pl
from jax.experimental.pallas import tpu as pltpu
from jax.sharding import Mesh, PartitionSpec as P

SPECIES = 8
RADIAL = 8
FACTORS = 4
CHANNELS = 64
K_SPEC = 12544
MAXAT = 16
ITERS = 4
K = 100352
STRUCTS = 256

LANES = 128
WIDTH = 896
PER_SPEC = K_SPEC // WIDTH
LOCAL = 8
BLOCK = LOCAL * MAXAT
PACKED = 72
CODE, COUNT, ENERGY = 64, 65, 66
GROUP = 128
FLAGS = 16

STRUCT = ("chip", "core")
CUTOFF = 5.0
PI_HIGH = 3.140625
PI_MID = 0.0009670257568359375
PI_LOW = math.pi - PI_HIGH - PI_MID
COS_TERMS = tuple((-1.0) ** n / math.factorial(2 * n) for n in range(9))


def cosine(angle):
    turns = jnp.floor(angle * (1.0 / math.pi) + 0.5)
    rest = angle - turns * PI_HIGH
    rest = rest - turns * PI_MID
    rest = rest - turns * PI_LOW
    square = rest * rest
    value = jnp.full_like(square, COS_TERMS[-1])
    for term in COS_TERMS[-2::-1]:
        value = value * square + term
    odd = turns - 2.0 * jnp.floor(turns * 0.5)
    return value * (1.0 - 2.0 * odd)


def atomic_kernel(dist_ref, nbr_ref, species_ref, counts_ref, pattern_ref, energies_ref, out_ref):
    ratio = dist_ref[...] / CUTOFF
    envelope = (1.0 - ratio) * (1.0 - ratio)
    nbr = nbr_ref[...]
    species = species_ref[...]
    radial = []
    for order in range(RADIAL):
        if order == 0:
            radial.append(envelope)
        else:
            radial.append(envelope * cosine((jnp.float32(math.pi) * jnp.float32(order)) * ratio))
    lane = lax.broadcasted_iota(jnp.int32, (SPECIES, LANES), 1)
    row = lax.broadcasted_iota(jnp.int32, (SPECIES, LANES), 0)
    center = jnp.where(species == row, 1.0, 0.0).astype(jnp.bfloat16)
    pattern = pattern_ref[...].astype(jnp.float32).astype(jnp.bfloat16)
    allowed = lax.dot_general(pattern, center, (((0,), (0,)), ((), ())), preferred_element_type=jnp.float32)
    rows = []
    for element in range(SPECIES):
        match = jnp.where(nbr == element, allowed[element : element + 1], 0.0)
        for order in range(RADIAL):
            rows.append(jnp.sum(match * radial[order], axis=0, keepdims=True))
    atomic = jnp.concatenate(rows, axis=0).astype(jnp.bfloat16)

    small = [counts_ref[...].astype(jnp.float32)]
    energy = energies_ref[...]
    for _ in range(3):
        small.append(energy.astype(jnp.bfloat16).astype(jnp.float32))
        energy = energy - small[-1]
    small = jnp.concatenate(small + [jnp.zeros((4, LOCAL), jnp.float32)], axis=0).astype(jnp.bfloat16)
    spots = jnp.concatenate([lane // MAXAT == row, lane == row], axis=1)
    small = jnp.dot(small, jnp.where(spots, 1.0, 0.0).astype(jnp.bfloat16), preferred_element_type=jnp.float32)
    slots = (lane[:1] % MAXAT).astype(jnp.float32)
    code = jnp.where(slots < small[:1, :LANES], species, SPECIES).astype(jnp.float32)
    parts = [code, small[:4, LANES:]]
    parts.append(jnp.zeros((PACKED - CHANNELS - 5, LANES), jnp.float32))
    packed = jnp.concatenate([atomic, jnp.concatenate(parts, axis=0).astype(jnp.bfloat16)], axis=0)
    for copy in range(out_ref.shape[0]):
        out_ref[copy, :, :] = packed


def atomic_call(dist, nbr_species, species, counts, pattern, energies, copies):
    vmem = pl.BlockSpec(memory_space=pltpu.VMEM)
    return pl.pallas_call(
        atomic_kernel,
        out_shape=jax.ShapeDtypeStruct((copies, PACKED, LANES), jnp.bfloat16),
        in_specs=[vmem] * 6,
        out_specs=vmem,
        name="atomic",
    )(dist, nbr_species, species.reshape(1, -1), counts.reshape(1, -1), pattern, energies.reshape(1, -1))


def maps_kernel(maps_ref, out_ref):
    for left in range(0, WIDTH, LANES):
        for factor in range(FACTORS):
            turned = maps_ref[factor, :, left : left + LANES].astype(jnp.float32).T.astype(jnp.bfloat16)
            for half in range(LANES // GROUP):
                row = ((left // GROUP + half) * FACTORS + factor) * GROUP
                out_ref[row : row + GROUP, :] = turned[half * GROUP : (half + 1) * GROUP]


def maps_call(maps):
    vmem = pl.BlockSpec(memory_space=pltpu.VMEM)
    return pl.pallas_call(
        maps_kernel,
        out_shape=jax.ShapeDtypeStruct((FACTORS * WIDTH, CHANNELS), jnp.bfloat16),
        in_specs=[vmem],
        out_specs=vmem,
        compiler_params=pltpu.CompilerParams(vmem_limit_bytes=8 * 1024 * 1024),
        cost_estimate=pl.CostEstimate(flops=0, bytes_accessed=1400000, transcendentals=0),
        name="maps",
    )(maps)


def place():
    core, chips = lax.axis_index("core"), lax.axis_size("chip")
    struct = lax.axis_index("chip") * 2 + core
    owners = SPECIES // lax.axis_size("basis") * PER_SPEC
    element = lax.div(lax.axis_index("basis") * owners + struct, PER_SPEC)
    return core, core * chips + lax.axis_index("chip"), jnp.where(struct < owners, element, SPECIES + 1)


def share_out(element, atoms_ref):
    codes = atoms_ref[:, CODE, :].astype(jnp.float32)
    lane = lax.broadcasted_iota(jnp.int32, codes.shape, 1)
    slot, structure = lane % MAXAT, (lane // MAXAT).astype(jnp.float32)
    chosen = jnp.where(codes == element, 1.0, 0.0)
    upto, since = chosen, chosen
    for reach in (1, 2, 4, 8):
        upto = upto + jnp.where(slot >= reach, pltpu.roll(upto, reach, 1), 0.0)
        since = since + jnp.where(slot < MAXAT - reach, pltpu.roll(since, LANES - reach, 1), 0.0)
    amount = upto + since - chosen
    partner = pltpu.roll(amount, codes.shape[0] // 2, 0)
    held = jnp.floor((amount + partner + 1.0) * 0.5)
    rank = upto - 1.0
    stays = jnp.where((chosen > 0.0) & (rank < held), rank * LOCAL + structure, -1.0)
    leaves = jnp.where((chosen > 0.0) & (rank >= held), (partner + rank - held) * LOCAL + structure, -1.0)
    return stays.astype(jnp.bfloat16), leaves.astype(jnp.bfloat16), held


def move_atoms(stays, leaves, atoms_ref, ranked_ref):
    chips = atoms_ref.shape[0]
    rows = lax.broadcasted_iota(jnp.int32, (BLOCK, LANES), 0).astype(jnp.float32).astype(jnp.bfloat16)
    one, zero = jnp.ones(rows.shape, jnp.bfloat16), jnp.zeros(rows.shape, jnp.bfloat16)
    flags = jnp.concatenate([one[:FLAGS], zero[:FLAGS]], axis=1)

    def hits(target):
        return jnp.where(jnp.broadcast_to(target, rows.shape) == rows, one, zero)

    for chip in range(0, chips, 2):
        pair = []
        for to in (chip, chip + 1):
            source = (to + chips // 2) % chips
            move = jnp.concatenate([hits(stays[to : to + 1, :]), hits(leaves[source : source + 1, :])], axis=1)
            atoms = jnp.concatenate([atoms_ref[to, :CHANNELS, :], atoms_ref[source, :CHANNELS, :]], axis=1)
            atoms = jnp.concatenate([atoms, flags], axis=0)
            pair.append(lax.dot_general(move, atoms, (((1,), (1,)), ((), ())), preferred_element_type=jnp.float32))
        for rank in range(MAXAT):
            tile = jnp.concatenate([moved[rank * LOCAL : (rank + 1) * LOCAL] for moved in pair], axis=0)
            ranked_ref[rank, chip * LOCAL : (chip + 2) * LOCAL, :] = tile.astype(jnp.bfloat16)


def ranked_kernel(own_ref, ranked_ref):
    stays, leaves, _ = share_out(place()[2].astype(jnp.float32), own_ref)
    move_atoms(stays, leaves, own_ref, ranked_ref)


def ranked_call(own):
    vmem = pl.BlockSpec(memory_space=pltpu.VMEM)
    return pl.pallas_call(
        ranked_kernel,
        out_shape=jax.ShapeDtypeStruct((MAXAT, own.shape[0] * LOCAL, CHANNELS + FLAGS), jnp.bfloat16),
        in_specs=[vmem],
        out_specs=vmem,
        compiler_params=pltpu.CompilerParams(vmem_limit_bytes=8 * 1024 * 1024),
        cost_estimate=pl.CostEstimate(flops=40000000, bytes_accessed=1400000, transcendentals=0),
        name="ranked",
    )(own)


def design_kernel(own_ref, other_ref, first_ref, maps_ref, high_ref, low_ref, gram_ref, second_ref, design_ref, crossed_ref):
    core, _, element = place()
    element = element.astype(jnp.float32)
    stays, leaves, held = share_out(element, other_ref)
    ranks = jnp.max(jnp.maximum(held, share_out(element, own_ref)[2])).astype(jnp.int32)
    move_atoms(stays, leaves, other_ref, second_ref)
    over = (((1,), (1,)), ((), ()))
    pick = lax.broadcasted_iota(jnp.int32, (16, CHANNELS + FLAGS), 1) == CHANNELS
    pick = jnp.where(pick, 1.0, 0.0).astype(jnp.bfloat16)

    def terms(atoms, left):
        columns = maps_ref[left * FACTORS : (left + GROUP) * FACTORS, :]
        values = lax.dot_general(columns, atoms, over, preferred_element_type=jnp.float32)
        product = values[:GROUP]
        for factor in range(1, FACTORS):
            product = product * values[factor * GROUP : (factor + 1) * GROUP]
        return product

    def add_ranks(first, amount, fresh):
        atoms = []
        for rank in range(amount):
            own, other = first_ref[first + rank], second_ref[first + rank]
            halves = [jnp.where(core == 0, own, other), jnp.where(core == 0, other, own)]
            operand = jnp.concatenate(halves, axis=0)
            flag = lax.dot_general(pick, operand, over, preferred_element_type=jnp.float32)
            mine = jnp.broadcast_to(flag[:1], (GROUP, STRUCTS)) > 0.5
            atoms.append((operand[:, :CHANNELS], mine))
        for left in range(0, WIDTH, GROUP):
            kept = crossed = None
            for operand, mine in atoms:
                product = terms(operand, left)
                here, there = jnp.where(mine, product, 0.0), jnp.where(mine, 0.0, product)
                kept = here if kept is None else kept + here
                crossed = there if crossed is None else crossed + there
            rows = slice(left, left + GROUP)
            design_ref[rows, :] = kept if fresh else design_ref[rows, :] + kept
            crossed_ref[rows, :] = crossed if fresh else crossed_ref[rows, :] + crossed

    odd = ranks % 4

    @pl.when(odd == 0)
    def _():
        design_ref[...] = jnp.zeros(design_ref.shape, jnp.float32)
        crossed_ref[...] = jnp.zeros(crossed_ref.shape, jnp.float32)

    for amount in range(1, 4):

        @pl.when(odd == amount)
        def _():
            add_ranks(0, amount, True)

    def add_fours(turn, carry):
        add_ranks(odd + turn * 4, 4, False)
        return carry

    lax.fori_loop(0, ranks // 4, add_fours, 0)
    crossed = [pltpu.roll(crossed_ref[:, at : at + LANES], LANES // 2, 1) for at in range(0, STRUCTS, LANES)]
    design = design_ref[...] + jnp.concatenate(crossed, axis=1)
    high = design.astype(jnp.bfloat16)
    low = (design - high.astype(jnp.float32)).astype(jnp.bfloat16)
    high_ref[...] = high
    low_ref[...] = low
    down = (((0,), (0,)), ((), ()))
    gram = lax.dot_general(high, high, down, preferred_element_type=jnp.float32)
    gram += lax.dot_general(high, low, down, preferred_element_type=jnp.float32)
    gram += lax.dot_general(low, high, down, preferred_element_type=jnp.float32)
    for left in range(0, STRUCTS, LANES):
        gram_ref[left // LANES * STRUCTS : (left // LANES + 1) * STRUCTS, :] = gram[:, left : left + LANES]


def design_call(own, other, ranked, maps):
    vmem = pl.BlockSpec(memory_space=pltpu.VMEM)
    return pl.pallas_call(
        design_kernel,
        out_shape=(
            jax.ShapeDtypeStruct((WIDTH, STRUCTS), jnp.bfloat16),
            jax.ShapeDtypeStruct((WIDTH, STRUCTS), jnp.bfloat16),
            jax.ShapeDtypeStruct((STRUCTS * STRUCTS // LANES, LANES), jnp.float32),
        ),
        in_specs=[vmem] * 4,
        out_specs=(vmem, vmem, vmem),
        scratch_shapes=[
            pltpu.VMEM((MAXAT, STRUCTS // 2, CHANNELS + FLAGS), jnp.bfloat16),
            pltpu.VMEM((WIDTH, STRUCTS), jnp.float32),
            pltpu.VMEM((WIDTH, STRUCTS), jnp.float32),
        ],
        compiler_params=pltpu.CompilerParams(vmem_limit_bytes=24 * 1024 * 1024),
        name="design",
    )(own, other, ranked, maps)


def total_kernel(parts_ref, out_ref):
    parts = parts_ref[...]
    out_ref[...] = jnp.broadcast_to(jnp.sum(parts, axis=0, keepdims=True), parts.shape)


def total_call(parts):
    vmem = pl.BlockSpec(memory_space=pltpu.VMEM)
    return pl.pallas_call(
        total_kernel,
        out_shape=jax.ShapeDtypeStruct(parts.shape, parts.dtype),
        in_specs=[vmem],
        out_specs=vmem,
        compiler_params=pltpu.CompilerParams(vmem_limit_bytes=4 * 1024 * 1024),
        name="total",
    )(parts)


def split(value, amount):
    parts = []
    for _ in range(amount):
        part = value.astype(jnp.bfloat16)
        parts.append(part)
        value = value - part.astype(jnp.float32)
    return parts


def stacked(vector):
    first, second, third = [part.astype(jnp.float32) for part in split(vector, 3)]
    row = lax.broadcasted_iota(jnp.int32, (16, vector.shape[1]), 0)
    one = jnp.where(row == 0, first, 0.0)
    two = jnp.where(row == 1, second, one)
    three = jnp.where(row == 2, third, two)
    return [operand.astype(jnp.bfloat16) for operand in (three, two)]


def picked(own_ref, other_ref, core):
    chips = own_ref.shape[0]
    kinds = (COUNT, ENERGY, ENERGY + 1, ENERGY + 2)
    parts = [half[:, kind, :].astype(jnp.float32) for kind in kinds for half in (own_ref, other_ref)]
    parts = jnp.concatenate(parts, axis=0).astype(jnp.bfloat16)
    structure = lax.broadcasted_iota(jnp.int32, (LANES, STRUCTS), 1)
    repeat = structure % LOCAL == lax.broadcasted_iota(jnp.int32, (LANES, STRUCTS), 0)
    parts = jnp.dot(parts, jnp.where(repeat, 1.0, 0.0).astype(jnp.bfloat16), preferred_element_type=jnp.float32)
    block = lax.broadcasted_iota(jnp.int32, (2 * chips, STRUCTS), 0)
    block = block % chips + jnp.where(block < chips, core, 1 - core) * chips
    here = block == lax.broadcasted_iota(jnp.int32, (2 * chips, STRUCTS), 1) // LOCAL
    rows = [
        jnp.sum(jnp.where(here, parts[kind * 2 * chips : (kind + 1) * 2 * chips], 0.0), axis=0, keepdims=True)
        for kind in range(len(kinds))
    ]
    return rows[0], rows[1] + rows[2] + rows[3]


def solve_kernel(gram_ref, own_ref, other_ref, high_ref, low_ref, coefficients_ref, direction_ref):
    core, number, _ = place()
    counts, energies = picked(own_ref, other_ref, core)
    inverse = 1.0 / counts
    gram = split(jnp.concatenate([gram_ref[:STRUCTS, :], gram_ref[STRUCTS:, :]], axis=1), 2)

    def dot(a, b):
        return jnp.sum(a * b, axis=1, keepdims=True)

    def apply(vector):
        image = jnp.zeros((16, STRUCTS), jnp.float32)
        for operand, part in zip(stacked(vector * inverse), gram):
            image = image + jnp.dot(operand, part, preferred_element_type=jnp.float32)
        return jnp.sum(image, axis=0, keepdims=True) * inverse

    image = apply(energies)
    square = dot(energies, energies)
    shrink = lax.rsqrt(square)
    beta = square * shrink
    left = energies * shrink
    right = left
    image = image * shrink
    square = dot(right, image)
    shrink = lax.rsqrt(square)
    alpha = square * shrink
    right, image = right * shrink, image * shrink
    search, search_image = right, image
    iterate = jnp.zeros_like(right)
    iterate_image = iterate
    phibar = beta
    rhobar = alpha
    for step in range(ITERS):
        left = image - alpha * left
        left_image = apply(left) if step < ITERS - 1 else None
        square = dot(left, left)
        shrink = lax.rsqrt(square)
        beta = square * shrink
        left = left * shrink
        over_rho = lax.rsqrt(rhobar * rhobar + square)
        cosine_part = rhobar * over_rho
        sine_part = beta * over_rho
        advance = cosine_part * phibar * over_rho
        phibar = sine_part * phibar
        iterate = iterate + advance * search
        iterate_image = iterate_image + advance * search_image
        if step < ITERS - 1:
            right = left - beta * right
            image = left_image * shrink - beta * image
            square = dot(right, image)
            shrink = lax.rsqrt(square)
            alpha = square * shrink
            right, image = right * shrink, image * shrink
            turn = sine_part * alpha * over_rho
            rhobar = -cosine_part * alpha
            search = right - turn * search
            search_image = image - turn * search_image
    iterate = iterate * (math.sqrt(K) * lax.rsqrt(dot(iterate, iterate_image))) * inverse
    over = (((1,), (1,)), ((), ()))
    values = jnp.zeros((16, WIDTH), jnp.float32)
    for operand, part in zip(stacked(iterate), (high_ref[...], low_ref[...])):
        values = values + lax.dot_general(operand, part, over, preferred_element_type=jnp.float32)
    values = jnp.sum(values, axis=0, keepdims=True)
    rows = jnp.concatenate([values[:, at : at + LANES] for at in range(0, WIDTH, LANES)], axis=0)
    for copy in range(coefficients_ref.shape[0]):
        coefficients_ref[copy] = rows
    direction = jnp.broadcast_to(left * math.sqrt(STRUCTS), (8, STRUCTS))
    direction_ref[...] = pltpu.roll(direction, lax.rem(STRUCTS - number * LOCAL, STRUCTS), 1)[:1, :LOCAL]


def solve_call(gram, own, other, high, low, copies):
    vmem = pl.BlockSpec(memory_space=pltpu.VMEM)
    return pl.pallas_call(
        solve_kernel,
        out_shape=(
            jax.ShapeDtypeStruct((copies, WIDTH // LANES, LANES), jnp.float32),
            jax.ShapeDtypeStruct((1, LOCAL), jnp.float32),
        ),
        in_specs=[vmem] * 5,
        out_specs=(vmem, vmem),
        compiler_params=pltpu.CompilerParams(vmem_limit_bytes=16 * 1024 * 1024),
        name="solve",
    )(gram, own, other, high, low)


def swap(value):
    return lax.ppermute(value, "core", [(0, 1), (1, 0)])


def body(dist, nbr_species, species, counts, pattern, projections, energies):
    struct = lax.axis_index(STRUCT)
    structs = lax.axis_size(STRUCT)
    owners = projections.shape[2] // WIDTH
    mine = jnp.minimum(struct, owners - 1)

    packed = atomic_call(dist, nbr_species, species, counts, pattern, energies, lax.axis_size("chip"))
    own = lax.all_to_all(packed, "chip", 0, 0)
    maps = maps_call(lax.dynamic_slice_in_dim(projections, mine * WIDTH, WIDTH, 2))
    own, maps = lax.optimization_barrier((own, maps))
    other = swap(own)
    ranked = ranked_call(own)
    high, low, gram = design_call(own, other, ranked, maps)
    everyone = ("chip", "core", "basis")
    parts = lax.all_to_all(gram.reshape(lax.axis_size(everyone), -1, LANES), everyone, 0, 0)
    gram = lax.all_to_all(total_call(parts), everyone, 0, 0).reshape(-1, LANES)
    values, direction = solve_call(gram, own, other, high, low, structs)
    values = lax.all_to_all(values, STRUCT, 0, 0)
    return (values[:owners].reshape(-1), direction.reshape(-1))


def solution(mesh):
    chips = Mesh(mesh.devices.reshape(-1, 2, mesh.shape["basis"]), ("chip", "core", "basis"))
    placed = (
        P(None, STRUCT),
        P(None, STRUCT),
        P(STRUCT),
        P(STRUCT),
        P(),
        P(None, None, "basis"),
        P(STRUCT),
    )
    return jax.shard_map(
        body, mesh=chips, in_specs=placed, out_specs=(P("basis"), P(STRUCT)), check_vma=False
    )
```
